256 devices in a mesh: seq: 16 (over y_hi, z), dp: 16 (over y_lo, x, core).
Axes of the slice: x: 4, y: 4 (y_hi: 2, y_lo: 2; y = y_hi * 2 + y_lo), z: 8, core: 2. Of those that a mesh axis runs over, the one named last changes fastest.
Arguments:
- byte_ids: int32 [16, 4096], P('dp', 'seq'), may hold values from 0 to 255
- embedding: bfloat16 [256, 1024], replicated, may hold values from -6 to 6
- gain: float32 [1024], replicated, may hold values from 0.5 to 1.5
- w_query: bfloat16 [1024, 1024], replicated, may hold values from -2 to 2
- w_key: bfloat16 [1024, 1024], replicated, may hold values from -2 to 2
- w_value: bfloat16 [1024, 1024], replicated, may hold values from -0.1875 to 0.1875
- w_out: bfloat16 [1024, 1024], replicated, may hold values from -0.1875 to 0.1875
- d_output: bfloat16 [16, 4096, 1024], P('dp', 'seq'), may hold values from -0.03125 to 0.03125
Outputs:
- d_key_weight: float32 [1024, 1024], P(('seq', 'dp'))
- d_gain: float32 [1024], P(('seq', 'dp'))
- d_embedding: float32 [256, 1024], P(('seq', 'dp'))
The draws below stay inside these ranges and needn't reach their ends.
All inputs are finite; a program needn't handle non-finite values.
Results may differ from the reference program's by a relative error of at most 0.0083.
Values may be sent and summed in bfloat16 or wider, within the bound.
No kernel may reach another device: no remote copies, remote signals or barrier semaphores. Data moves between devices by JAX's collectives and lax.ppermute only.
A program may use at most 128 MiB of HBM per device.

```python
import math
import jax
import jax.numpy as jnp
import numpy as np
from jax import lax

D = 1024
HEADS = 8
HEAD_DIM = 128
VOCAB = 256
TOK_DEV = 256
WINDOW = 256
LENGTH = 4096
BATCH = 16
N_SEQ = 16
N_DP = 16


def weight_pair(key):
    shape = (D, HEADS * HEAD_DIM)
    base_query = jnp.clip(jax.random.normal(jax.random.fold_in(key, 11), shape, jnp.float32), -6.0, 6.0)
    base_key = jnp.clip(jax.random.normal(jax.random.fold_in(key, 12), shape, jnp.float32), -6.0, 6.0)
    factor_all = D ** (-0.5)
    return (base_query * factor_all, base_key * factor_all)


def draw_w_query(key, part):
    return weight_pair(key)[0].astype(jnp.bfloat16)


def draw_w_key(key, part):
    return weight_pair(key)[1].astype(jnp.bfloat16)


def touch_ends(array, stream_key, low, high):
    longest = array.shape.index(max(array.shape))
    spots = []
    for shift in (0, 1):
        where = [jax.random.randint(jax.random.fold_in(stream_key, axis), (), 0, length) for axis, length in enumerate(array.shape)]
        where[longest] = (where[longest] + shift) % array.shape[longest]
        spots.append(tuple(where))
    return array.at[spots[0]].set(low).at[spots[1]].set(high)


def raised(drawn, rng, source, target, parts, factor):
    def block_of(dim):
        return (jnp.arange(drawn.shape[dim]) // (drawn.shape[dim] // parts)).reshape((-1,) + (1,) * (drawn.ndim - 1 - dim))

    near = jax.random.permutation(rng, parts)[block_of(target)]
    far = (block_of(target) + parts // 2) % parts
    return jnp.where((block_of(source) == near) | (block_of(source) == far), factor * drawn, drawn)


def block_scale(stream_key, shape, split, least, top_value):
    level, own = 1.0, jax.random.fold_in(stream_key, 6)
    for dim, parts in split:
        heights = jnp.exp(jax.random.uniform(jax.random.fold_in(own, dim), (parts,), jnp.float32, least / len(split), top_value / len(split)))
        level = level * jnp.repeat(heights, shape[dim] // parts).reshape([-1 if axis == dim else 1 for axis in range(len(shape))])
    return level


def rank_table(count, slope):
    portions = [(1 << 20) // math.isqrt(rank ** slope) + 1 for rank in range(1, count + 1)]
    deviation = 1 + sum(portions) // (1 << 30)
    return np.cumsum(np.array([max(1, weight // deviation) for weight in portions]))


def skewed_ids(stream_key, dims, count, slope):
    table = rank_table(count, slope)
    pick = jax.random.randint(jax.random.fold_in(stream_key, 1), dims, 0, int(table[count - 1]))
    grade = jnp.searchsorted(jnp.asarray(table, jnp.int32), pick, side="right")
    return jax.random.permutation(jax.random.fold_in(stream_key, 2), count)[grade].astype(jnp.int32)


def gaussian(rng, dims, width, bound, split=(), kind=jnp.bfloat16):
    level = block_scale(rng, dims, split, -0.22, 0.18) if split else 1.0
    array = jax.random.normal(rng, dims, jnp.float32) * width * level
    return jnp.minimum(jnp.maximum(array, -bound), bound).astype(kind)


def heavy_noise(stream_key, shape, scale, bound, pieces, heavy, kind=jnp.bfloat16):
    result = scale * jax.random.normal(stream_key, shape, jnp.float32)
    if pieces:
        result = result * block_scale(stream_key, shape, pieces, -0.22, 0.18)
    return jnp.clip(raised(result, jax.random.fold_in(stream_key, 3), *heavy), -bound, bound).astype(kind)


def setup_inputs(seed: int = 0) -> dict:
    arg_keys = jax.random.split(jax.random.key(seed), 9)
    return {
        "byte_ids": touch_ends(skewed_ids(arg_keys[0], (BATCH, LENGTH), VOCAB, 2), jax.random.fold_in(arg_keys[0], 3), 0, VOCAB - 1).astype(jnp.int32),
        "embedding": gaussian(arg_keys[1], (VOCAB, D), 1.0, 6.0),
        "gain": jnp.clip(1.0 + 0.1 * jax.random.normal(arg_keys[2], (D,), jnp.float32), 0.5, 1.5),
        "w_query": draw_w_query(jax.random.fold_in(arg_keys[8], 71), 0),
        "w_key": draw_w_key(jax.random.fold_in(arg_keys[8], 71), 0),
        "w_value": gaussian(arg_keys[5], (D, HEADS * HEAD_DIM), D ** -0.5, 0.1875),
        "w_out": gaussian(arg_keys[6], (D, HEADS * HEAD_DIM), (HEADS * HEAD_DIM) ** -0.5, 0.1875),
        "d_output": heavy_noise(arg_keys[7], (BATCH, LENGTH, D), ((TOK_DEV * N_SEQ * N_DP) ** -0.5), 0.03125, ((0, 16), (1, 16)), (1, 2, 16, 2.0)),
    }


NEGATIVE = -1e+30
EPSILON = 1e-05
THETA = 10000.0

def tables(position, half_dim):
    inverse = THETA ** (-jnp.arange(half_dim, dtype=jnp.float32) / half_dim)
    angles = position.astype(jnp.float32)[:, None] * inverse[None, :]
    return (jnp.cos(angles), jnp.sin(angles))

def rotate(matrix, cosine, sine_table, head_count, direction):
    row_count = matrix.shape[0]
    per_head = matrix.reshape(row_count, head_count, -1)
    half_dim = per_head.shape[-1] // 2
    former = per_head[..., :half_dim]
    latter = per_head[..., half_dim:]
    cos_part = cosine[:, None, :]
    sin_part = direction * sine_table[:, None, :]
    joined = jnp.concatenate([former * cos_part - latter * sin_part, latter * cos_part + former * sin_part], axis=-1)
    return joined.reshape(row_count, -1)

def product(left_op, right_op):
    return jnp.dot(left_op, right_op, preferred_element_type=jnp.float32)

def contract(left_op, right_op):
    return lax.dot_general(left_op, right_op, (((0,), (0,)), ((), ())), preferred_element_type=jnp.float32)

def against(left_op, right_op):
    return lax.dot_general(left_op, right_op, (((1,), (1,)), ((), ())), preferred_element_type=jnp.float32)

def band_attention(queries, key_cat, value_cat, grad_out, w_out, leading, head_count):
    row_count, feat_width = queries.shape
    head_dim = feat_width // head_count
    score_scale = head_dim ** (-0.5)
    query_h = queries.reshape(row_count, head_count, head_dim).astype(jnp.float32)
    key_h = key_cat.reshape(2 * row_count, head_count, head_dim).astype(jnp.float32)
    value_h = value_cat.reshape(2 * row_count, head_count, head_dim).astype(jnp.float32)
    scores = jnp.einsum('qhd,khd->hqk', query_h, key_h) * score_scale
    row_pos = jnp.arange(row_count, dtype=jnp.int32)[:, None]
    col_pos = jnp.arange(2 * row_count, dtype=jnp.int32)[None, :]
    allowed = (col_pos > row_pos) & (col_pos <= row_pos + row_count) & ((col_pos >= row_count) | jnp.logical_not(leading))
    scores = jnp.where(allowed[None], scores, NEGATIVE)
    highest = lax.optimization_barrier(jnp.max(scores, axis=-1, keepdims=True))
    weights = jnp.exp(scores - highest)
    probability = weights / lax.optimization_barrier(jnp.sum(weights, axis=-1, keepdims=True))
    rounded = lax.optimization_barrier(probability.astype(jnp.bfloat16)).astype(jnp.float32)
    grad_att = product(grad_out, w_out).astype(jnp.bfloat16)
    grad_h = grad_att.reshape(row_count, head_count, head_dim).astype(jnp.float32)
    grad_probs = jnp.einsum('qhd,khd->hqk', grad_h, value_h)
    grad_values = jnp.einsum('hqk,qhd->khd', rounded, grad_h).reshape(2 * row_count, feat_width)
    row_delta = lax.optimization_barrier(jnp.sum(probability * grad_probs, axis=-1, keepdims=True))
    grad_scores = lax.optimization_barrier((probability * (grad_probs - row_delta) * score_scale).astype(jnp.bfloat16)).astype(jnp.float32)
    grad_queries = jnp.einsum('hqk,khd->qhd', grad_scores, key_h).reshape(row_count, feat_width)
    grad_keys = jnp.einsum('hqk,qhd->khd', grad_scores, query_h).reshape(2 * row_count, feat_width)
    return (grad_queries, grad_keys, grad_values)

def one_sequence(byte_row, grad_row, embedding, gain, w_query, w_key, w_value, w_out):
    length = byte_row.shape[0]
    window = WINDOW
    blocks = length // window
    hd_width = w_query.shape[1]
    half_dim = HEAD_DIM // 2
    inputs = embedding[byte_row].astype(jnp.float32)
    recip = lax.rsqrt(lax.optimization_barrier(jnp.mean(inputs * inputs, axis=-1, keepdims=True)) + EPSILON)
    normed = (inputs * recip * gain[None, :]).astype(jnp.bfloat16)
    places = jnp.arange(length, dtype=jnp.int32)
    cosine, sine_table = tables(places, half_dim)
    prev_cos, prev_sin = tables(places - window, half_dim)
    queries = rotate(product(normed, w_query), cosine, sine_table, HEADS, 1.0).astype(jnp.bfloat16)
    keys_all = rotate(product(normed, w_key), cosine, sine_table, HEADS, 1.0).astype(jnp.bfloat16)
    values_all = product(normed, w_value).astype(jnp.bfloat16)
    query_blk = queries.reshape(blocks, window, hd_width)
    key_blk = keys_all.reshape(blocks, window, hd_width)
    value_blk = values_all.reshape(blocks, window, hd_width)
    key_prev = jnp.concatenate([jnp.zeros_like(key_blk[:1]), key_blk[:-1]], axis=0)
    value_prev = jnp.concatenate([jnp.zeros_like(value_blk[:1]), value_blk[:-1]], axis=0)
    grad_blk = grad_row.reshape(blocks, window, -1)

    def per_block(item):
        index, query_b, key_b, key_p, value_b, value_p, grad_b = item
        return band_attention(query_b, jnp.concatenate([key_p, key_b], axis=0), jnp.concatenate([value_p, value_b], axis=0), grad_b, w_out, index == 0, HEADS)
    grad_q, grad_k, grad_v = lax.map(per_block, (jnp.arange(blocks, dtype=jnp.int32), query_blk, key_blk, key_prev, value_blk, value_prev, grad_blk))
    grad_query = rotate(grad_q.reshape(length, hd_width), cosine, sine_table, HEADS, -1.0).astype(jnp.bfloat16)
    key_own = rotate(grad_k[:, window:].reshape(length, hd_width), cosine, sine_table, HEADS, -1.0).astype(jnp.bfloat16)
    key_next = rotate(grad_k[:, :window].reshape(length, hd_width), prev_cos, prev_sin, HEADS, -1.0).astype(jnp.bfloat16)
    value_own = grad_v[:, window:].reshape(length, hd_width).astype(jnp.bfloat16)
    value_next = grad_v[:, :window].reshape(length, hd_width).astype(jnp.bfloat16)
    key_from = jnp.concatenate([key_next[window:], jnp.zeros_like(key_next[:window])], axis=0)
    value_from = jnp.concatenate([value_next[window:], jnp.zeros_like(value_next[:window])], axis=0)
    grad_wk = contract(normed, key_own) + contract(normed, key_from)
    grad_normed = against(grad_query, w_query) + against(key_own, w_key) + against(value_own, w_value) + against(key_from, w_key) + against(value_from, w_value)
    scaled = inputs * recip
    grad_gain = lax.optimization_barrier(jnp.sum(grad_normed * scaled, axis=0))
    grad_scaled = grad_normed * gain[None, :]
    grad_inputs = recip * grad_scaled - inputs * recip ** 3 * lax.optimization_barrier(jnp.mean(grad_scaled * inputs, axis=-1, keepdims=True))
    grad_table = jax.ops.segment_sum(grad_inputs, byte_row, num_segments=VOCAB)
    return (grad_wk, grad_gain, grad_table)

def reference(byte_ids, embedding, gain, w_query, w_key, w_value, w_out, d_output):
    hd_width = w_query.shape[1]
    start = (jnp.zeros((D, hd_width), jnp.float32), jnp.zeros((D,), jnp.float32), jnp.zeros((VOCAB, D), jnp.float32))

    def step(carry, item):
        terms = one_sequence(item[0], item[1], embedding, gain, w_query, w_key, w_value, w_out)
        return (jax.tree.map(jnp.add, carry, terms), None)
    total, _ = lax.scan(step, start, (byte_ids, d_output))
    return (total[0], total[1], total[2])
```

```python
import math

import jax
import jax.numpy as jnp
import numpy as np
from jax import lax
from jax.experimental import pallas as pl
from jax.experimental.pallas import tpu as pltpu
from jax.sharding import PartitionSpec as P

HEADS = 8
HEAD_DIM = 128
D = 1024
VOCAB = 256
TOK = 256
N_Z = 8
N_DP = 16
MEMBERS = 32
NEGATIVE = -1e30
EPSILON = 1e-05
THETA = 10000.0
AXES = ("seq", "dp")
BF = jnp.bfloat16
F32 = jnp.float32
VMEM_LIMIT = 56 * 1024 * 1024


def plane_groups():
    return [[(y * N_Z + z) * N_DP + d for y in range(2) for d in range(N_DP)] for z in range(N_Z)]


def ring_groups():
    return [[(y * N_Z + z) * N_DP + d for z in range(N_Z)] for y in range(2) for d in range(N_DP)]


def exchange(value, groups):
    return lax.all_to_all(value, AXES, 0, 0, axis_index_groups=groups, tiled=False)


def angle_tables():
    inverse = THETA ** (-np.arange(HEAD_DIM // 2, dtype=np.float64) / (HEAD_DIM // 2))
    near = np.arange(-TOK, TOK, dtype=np.float64)[:, None] * inverse[None, :]
    base = (TOK * np.arange(16, dtype=np.float64))[:, None] * inverse[None, :]

    def wide(angle):
        cosine, sine = np.cos(angle), np.sin(angle)
        return np.stack(
            [np.concatenate([cosine, cosine], -1), np.concatenate([-sine, sine], -1)]
        ).astype(np.float32)

    return wide(near), wide(base)


def mm(left, right):
    return lax.dot_general(left, right, (((1,), (0,)), ((), ())), preferred_element_type=F32)


def mm_nt(left, right):
    return lax.dot_general(left, right, (((1,), (1,)), ((), ())), preferred_element_type=F32)


def mm_tn(left, right):
    return lax.dot_general(left, right, (((0,), (0,)), ((), ())), preferred_element_type=F32)


def table_row(ids):
    return (ids & 128) | ((ids & 15) << 3) | ((ids >> 4) & 7)


def hot_columns(ids_row):
    place = lax.broadcasted_iota(jnp.int32, (VOCAB, TOK), 0)
    return (place == table_row(ids_row)).astype(F32).astype(BF)


def turn_tables(near_ref, base_ref, rows, block):
    near_c, near_s = near_ref[0, rows, :], near_ref[1, rows, :]
    base_c, base_s = base_ref[0, pl.ds(block, 1), :], base_ref[1, pl.ds(block, 1), :]
    return near_c * base_c - near_s * base_s, near_s * base_c + near_c * base_s


def turn(value, cosine, sine):
    return value * cosine + pltpu.roll(value, HEAD_DIM // 2, 1) * sine


def turn_back(value, cosine, sine):
    return value * cosine - pltpu.roll(value, HEAD_DIM // 2, 1) * sine


def head(index):
    return slice(index * HEAD_DIM, (index + 1) * HEAD_DIM)


def project_kernel(
    ids_ref, gain_ref, near_ref, base_ref, emb_any, wk_any, wv_any, wq_any, do_any, wo_any,
    q_ref, k_ref, v_ref, ga_ref, ktab_ref, vtab_ref,
    emb, wk, wv, wq, do, wo, qtab, sems,
):
    pairs = [(emb_any, emb), (wk_any, wk), (wv_any, wv), (wq_any, wq), (do_any, do), (wo_any, wo)]
    copies = [pltpu.make_async_copy(s, d, sems.at[i]) for i, (s, d) in enumerate(pairs)]
    for copy in copies:
        copy.start()
    block = lax.axis_index("seq")
    hot = hot_columns(ids_ref[...])
    cosine, sine = turn_tables(near_ref, base_ref, slice(TOK, 2 * TOK), block)
    order = lax.broadcasted_iota(jnp.int32, (VOCAB, VOCAB), 0)
    value = (order & 128) | ((order & 7) << 4) | ((order >> 3) & 15)
    swap = (lax.broadcasted_iota(jnp.int32, (VOCAB, VOCAB), 1) == value).astype(F32).astype(BF)
    copies[0].wait()
    inputs = mm(swap, emb[...])
    recip = lax.rsqrt(jnp.mean(inputs * inputs, axis=-1, keepdims=True) + EPSILON)
    normed = (inputs * recip * gain_ref[...]).astype(BF)
    hot2 = jnp.concatenate([hot, hot], axis=0)

    def fill(tab_ref, weight):
        full = mm(normed, weight[...])
        high = full.astype(BF)
        tab_ref[:VOCAB, :] = high
        tab_ref[VOCAB:, :] = (full - high.astype(F32)).astype(BF)

    def gather(tab_ref, out_ref):
        full = mm_tn(hot2, tab_ref[...])
        for h in range(HEADS):
            out_ref[:, head(h)] = turn(full[:, head(h)], cosine, sine).astype(BF)

    copies[1].wait()
    fill(ktab_ref, wk)
    gather(ktab_ref, k_ref)
    copies[2].wait()
    vtab_ref[...] = mm(normed, wv[...]).astype(BF)
    v_ref[...] = mm_tn(hot, vtab_ref[...]).astype(BF)
    copies[3].wait()
    fill(qtab, wq)
    gather(qtab, q_ref)
    copies[4].wait()
    copies[5].wait()
    ga_ref[...] = mm(do[...], wo[...]).astype(BF)


def attend_kernel(
    ids_ref, prev_ref, near_ref, base_ref, q_ref, k_ref, v_ref, ga_ref, ktab_ref, vtab_ref,
    wq_any, wk_any, wv_any,
    out_ref,
    kprev, vprev, gq, kg, vg, wq, wk, wv, sems,
):
    pairs = [(wq_any, wq), (wk_any, wk), (wv_any, wv)]
    copies = [pltpu.make_async_copy(s, d, sems.at[i]) for i, (s, d) in enumerate(pairs)]
    for copy in copies:
        copy.start()
    block = lax.axis_index("seq")
    lead = jnp.where(block == 0, NEGATIVE, 0.0).astype(F32)
    hot_own = hot_columns(ids_ref[...])
    hot_prev = hot_columns(prev_ref[...])
    cos_p, sin_p = turn_tables(near_ref, base_ref, slice(0, TOK), block)
    cos_o, sin_o = turn_tables(near_ref, base_ref, slice(TOK, 2 * TOK), block)
    full = mm_tn(jnp.concatenate([hot_prev, hot_prev], axis=0), ktab_ref[...])
    for h in range(HEADS):
        kprev[:, head(h)] = turn(full[:, head(h)], cos_p, sin_p).astype(BF)
    vprev[...] = mm_tn(hot_prev, vtab_ref[...]).astype(BF)
    scale = HEAD_DIM ** (-0.5)
    own = lax.broadcasted_iota(jnp.int32, (TOK, TOK), 0) <= lax.broadcasted_iota(
        jnp.int32, (TOK, TOK), 1
    )
    for h in range(HEADS):
        query, grad = q_ref[:, head(h)], ga_ref[:, head(h)]
        key_o, key_p = k_ref[:, head(h)], kprev[:, head(h)]
        value_o, value_p = v_ref[:, head(h)], vprev[:, head(h)]
        scores = jnp.where(own, mm_nt(key_o, query), mm_nt(key_p, query) + lead)
        highest = jnp.max(scores, axis=0, keepdims=True)
        weights = jnp.exp((scores - highest) * scale)
        probs = weights * (1.0 / jnp.sum(weights, axis=0, keepdims=True))
        grad_probs = jnp.where(own, mm_nt(value_o, grad), mm_nt(value_p, grad))
        delta = jnp.sum(probs * grad_probs, axis=0, keepdims=True)
        grad_scores = probs * (grad_probs - delta) * scale
        probs_o = jnp.where(own, probs, 0.0).astype(BF)
        probs_p = jnp.where(own, 0.0, probs).astype(BF)
        gs_o = jnp.where(own, grad_scores, 0.0).astype(BF)
        gs_p = jnp.where(own, 0.0, grad_scores).astype(BF)
        vg[:TOK, head(h)] = mm(probs_p, grad).astype(BF)
        vg[TOK:, head(h)] = mm(probs_o, grad).astype(BF)
        kg[:TOK, head(h)] = turn_back(mm(gs_p, query), cos_p, sin_p).astype(BF)
        kg[TOK:, head(h)] = turn_back(mm(gs_o, query), cos_o, sin_o).astype(BF)
        grad_q = mm_tn(gs_o, key_o) + mm_tn(gs_p, key_p)
        gq[:, head(h)] = turn_back(grad_q, cos_o, sin_o).astype(BF)
    hot2 = jnp.concatenate([hot_prev, hot_own], axis=1)
    key_table = mm(hot2, kg[...]).astype(BF)
    out_ref[:, :D] = key_table
    value_table = mm(hot2, vg[...]).astype(BF)
    query_table = mm(hot_own, gq[...]).astype(BF)
    for copy in copies:
        copy.wait()
    grad_normed = mm_nt(query_table, wq[...]) + mm_nt(key_table, wk[...]) + mm_nt(value_table, wv[...])
    out_ref[:, D:] = grad_normed.astype(BF)


def rows_kernel(emb_ref, gain_ref, scaled_ref, pick_ref, row_ref, spread):
    block, lane = lax.axis_index("seq"), lax.axis_index("dp")
    high, ring = block // N_Z, lax.rem(block, N_Z)
    first = high * 128 + lane
    rows = lax.broadcasted_iota(jnp.int32, (8, VOCAB), 0) * 16 + first
    hot = (lax.broadcasted_iota(jnp.int32, (8, VOCAB), 1) == rows).astype(F32).astype(BF)
    inputs = mm(hot, emb_ref[...])
    recip = lax.rsqrt(jnp.mean(inputs * inputs, axis=-1, keepdims=True) + EPSILON)
    scaled = inputs * recip
    scaled_ref[...] = scaled
    normed = (scaled * gain_ref[...]).astype(BF)
    place = lax.broadcasted_iota(jnp.int32, (D, 256), 1)
    member = place >> 3
    column = ((member >> 4) << 9) + ring * 64 + ((member & 15) << 2) + (place & 3)
    choose = (lax.broadcasted_iota(jnp.int32, (D, 256), 0) == column).astype(F32).astype(BF)
    picked = mm(normed, choose)
    pick_ref[...] = jnp.concatenate([picked, picked], axis=0).astype(BF)
    for k in range(8):
        spread[:, k, :] = inputs[:, k * 128 : (k + 1) * 128]
    row_ref[...] = spread[ring]


def ring_kernel(got_ref, scaled_ref, out_ref, spread, terms):
    total = jnp.sum(got_ref[...].astype(F32), axis=0)
    key_part, grad_part = total[:, :D], total[:, D:]
    product = jnp.sum(grad_part * scaled_ref[...], axis=0, keepdims=True)
    for k in range(8):
        spread[:, k, :] = grad_part[:, k * 128 : (k + 1) * 128]
        terms[k : k + 1, :] = product[:, k * 128 : (k + 1) * 128]
    out_ref[:, :, :D] = jnp.broadcast_to(key_part.astype(BF)[None], (N_Z, 8, D))
    out_ref[:, :, D : D + 128] = spread[...].astype(BF)
    out_ref[:, :, D + 128 :] = jnp.broadcast_to(terms[...].astype(BF)[None], (N_Z, 8, 128))


def weight_kernel(got_ref, pick_ref, row_ref, gain_ref, out_ref, ge_ref):
    total = jnp.sum(got_ref[...].astype(F32), axis=0)
    keys = total[:, :D]
    high = keys.astype(BF).astype(F32)
    both = jnp.concatenate([high, keys - high], axis=0).astype(BF)
    part = mm_tn(pick_ref[...], both)
    first = (lax.broadcasted_iota(jnp.int32, (256, 512), 0) & 4) == 0
    part = jnp.where(first, part[:, :512], part[:, 512:])
    out_ref[:, :, :512] = part.reshape(MEMBERS, 8, 512).astype(BF)
    out_ref[:, :, 512:] = jnp.broadcast_to(total[:, D + 128 :].astype(BF)[None], (MEMBERS, 8, 128))
    grad_normed = total[:, D : D + 128]
    inputs = row_ref[...]

    def mean(value):
        return jnp.sum(jnp.sum(value, axis=1, keepdims=True), axis=0, keepdims=True) * (1.0 / D)

    recip = lax.rsqrt(mean(inputs * inputs) + EPSILON)
    grad_scaled = grad_normed * gain_ref[...]
    ge_ref[...] = recip * grad_scaled - inputs * (recip * recip * recip) * mean(grad_scaled * inputs)


def finish_kernel(got_ref, gk_ref, gg_ref):
    total = jnp.sum(got_ref[...].astype(F32), axis=0)
    gk_ref[:, :512] = total[:4, :512]
    gk_ref[:, 512:] = total[4:, :512]
    gg_ref[...] = total[:, 512:]


def call(kernel, outs, ins, scratch=(), flops=0, moved=0):
    any_space = pl.BlockSpec(memory_space=pl.ANY)
    vmem = pl.BlockSpec(memory_space=pltpu.VMEM)
    return pl.pallas_call(
        kernel,
        out_shape=[jax.ShapeDtypeStruct(shape, kind) for shape, kind in outs],
        in_specs=[any_space if far else vmem for _, far in ins],
        out_specs=[vmem] * len(outs),
        scratch_shapes=list(scratch),
        compiler_params=pltpu.CompilerParams(vmem_limit_bytes=VMEM_LIMIT),
        cost_estimate=pl.CostEstimate(flops=flops, bytes_accessed=moved, transcendentals=0),
    )(*[value for value, _ in ins])


def local(byte_ids, embedding, gain, w_query, w_key, w_value, w_out, d_output):
    near_table, base_table = (jnp.asarray(table) for table in angle_tables())
    block, lane = lax.axis_index("seq"), lax.axis_index("dp")
    prev_ids = lax.ppermute(byte_ids, "seq", [(i, i + 1) for i in range(15)])
    gain_row = gain.reshape(1, D)
    gain_tile = gain.reshape(8, 128)
    wide = ((TOK, D), BF)
    mat = pltpu.VMEM((D, D), BF)
    tall = pltpu.VMEM((2 * TOK, D), BF)
    flat = pltpu.VMEM((TOK, D), BF)
    near = lambda *values: [(value, False) for value in values]
    far = lambda *values: [(value, True) for value in values]
    q, k, v, ga, ktab, vtab = call(
        project_kernel,
        [wide, wide, wide, wide, ((2 * VOCAB, D), BF), wide],
        near(byte_ids, gain_row, near_table, base_table)
        + far(embedding, w_key, w_value, w_query, d_output[0], w_out),
        [flat, mat, mat, mat, flat, mat, tall, pltpu.SemaphoreType.DMA((6,))],
        flops=4_000_000_000,
        moved=14_000_000,
    )
    (tables,) = call(
        attend_kernel,
        [((VOCAB, 2 * D), BF)],
        near(byte_ids, prev_ids, near_table, base_table, q, k, v, ga, ktab, vtab)
        + far(w_query, w_key, w_value),
        [flat, flat, flat, tall, tall, mat, mat, mat, pltpu.SemaphoreType.DMA((3,))],
        flops=5_000_000_000,
        moved=12_000_000,
    )
    first = exchange(tables.reshape(MEMBERS, 8, 2 * D), plane_groups())
    embedding_later, _ = lax.optimization_barrier((embedding, tables))
    scaled, pick, row = call(
        rows_kernel,
        [((8, D), F32), ((16, 256), BF), ((8, 128), F32)],
        near(embedding_later, gain_row),
        [pltpu.VMEM((8, 8, 128), F32)],
        flops=10_000_000,
        moved=600_000,
    )
    (ring,) = call(
        ring_kernel,
        [((N_Z, 8, D + 256), BF)],
        near(first, scaled),
        [pltpu.VMEM((8, 8, 128), F32), pltpu.VMEM((8, 128), F32)],
        flops=1_000_000,
        moved=1_000_000,
    )
    second = exchange(ring, ring_groups())
    part, grad_row = call(
        weight_kernel,
        [((MEMBERS, 8, 640), BF), ((8, 128), F32)],
        near(second, pick, row, gain_tile),
        flops=10_000_000,
        moved=400_000,
    )
    third = exchange(part, plane_groups())
    gk, gg = call(
        finish_kernel,
        [((4, D), F32), ((8, 128), F32)],
        near(third),
        flops=1_000_000,
        moved=400_000,
    )
    gg_own = lax.dynamic_slice(gg.reshape(D), ((block * N_DP + lane) * 4,), (4,))
    return gk, gg_own, grad_row.reshape(1, D)


def solution(mesh):
    in_specs = (P("dp", "seq"), P(), P(), P(), P(), P(), P(), P("dp", "seq", None))
    out_specs = (P(("seq", "dp"), None), P(("seq", "dp")), P(("seq", "dp"), None))
    return jax.shard_map(local, mesh=mesh, in_specs=in_specs, out_specs=out_specs, check_vma=False)
```

```python
import jax
import jax.numpy as jnp
import numpy as np
from jax import lax
from jax.experimental import pallas as pl
from jax.experimental.pallas import tpu as pltpu
from jax.sharding import PartitionSpec as P

HEADS = 8
HEAD_DIM = 128
D = 1024
VOCAB = 256
TOK = 256
N = 16
NEGATIVE = -1e30
EPSILON = 1e-05
THETA = 10000.0
BF = jnp.bfloat16
F32 = jnp.float32
MIB = 1024 * 1024

PLANE = 32
RING = 8
WIDE = 2 * D + 256
ROUNDS = ((1,), (2,), (4,))


def exchange(value):
    groups = [[(y * RING + z) * N + d for y in range(2) for d in range(N)] for z in range(RING)]
    return lax.all_to_all(value, ("seq", "dp"), 0, 0, axis_index_groups=groups, tiled=False)


def swap(value, step):
    return lax.ppermute(value, "seq", [(i, i ^ step) for i in range(N)])


def angle_tables():
    inverse = THETA ** (-np.arange(HEAD_DIM // 2, dtype=np.float64) / (HEAD_DIM // 2))
    near = np.arange(-TOK, TOK, dtype=np.float64)[:, None] * inverse[None, :]
    base = (TOK * np.arange(16, dtype=np.float64))[:, None] * inverse[None, :]

    def wide(angle):
        cosine, sine = np.cos(angle), np.sin(angle)
        return np.stack(
            [np.concatenate([cosine, cosine], -1), np.concatenate([-sine, sine], -1)]
        ).astype(np.float32)

    return wide(near), wide(base)


def mm(left, right):
    return lax.dot_general(left, right, (((1,), (0,)), ((), ())), preferred_element_type=F32)


def mm_nt(left, right):
    return lax.dot_general(left, right, (((1,), (1,)), ((), ())), preferred_element_type=F32)


def mm_tn(left, right):
    return lax.dot_general(left, right, (((0,), (0,)), ((), ())), preferred_element_type=F32)


def table_row(ids):
    return (ids & 128) | ((ids & 15) << 3) | ((ids >> 4) & 7)


def hot_columns(ids_row):
    place = lax.broadcasted_iota(jnp.int32, (VOCAB, TOK), 0)
    return (place == table_row(ids_row)).astype(F32).astype(BF)


def turn_tables(near_ref, base_ref, rows, block):
    near_c, near_s = near_ref[0, rows, :], near_ref[1, rows, :]
    base_c, base_s = base_ref[0, pl.ds(block, 1), :], base_ref[1, pl.ds(block, 1), :]
    return near_c * base_c - near_s * base_s, near_s * base_c + near_c * base_s


def turn(value, cosine, sine):
    return value * cosine + pltpu.roll(value, HEAD_DIM // 2, 1) * sine


def turn_back(value, cosine, sine):
    return value * cosine - pltpu.roll(value, HEAD_DIM // 2, 1) * sine


def head(index):
    return slice(index * HEAD_DIM, (index + 1) * HEAD_DIM)


def split(value):
    high = value.astype(BF).astype(F32)
    return high, value - high


def tiles(value, scratch):
    for k in range(8):
        scratch[k : k + 1, :] = value[:, k * 128 : (k + 1) * 128]
    return scratch[...]


def halve(value, step, count, keep_ref, send_ref):
    bit = (lax.axis_index("seq") // step) % 2
    keep_ref[...] = value[pl.ds(pl.multiple_of(bit * count, count), count), :]
    send_ref[...] = value[pl.ds(pl.multiple_of((1 - bit) * count, count), count), :].astype(BF)


def tables_kernel(*refs):
    prev_ref, sources, (out_ref,) = refs[0], refs[1:11], refs[11:12]
    near_ref, base_ref, ids_ref, gain_ref, emb, wk, wv, wq, do, wo = refs[12:22]
    tab, q_ref, k_ref, v_ref, ga_ref, kprev, vprev, vtab, gq, kg, vg, sems = refs[22:]
    kept = (emb, near_ref, base_ref, ids_ref, gain_ref, wk, wv, wq, do, wo)
    copies = [pltpu.make_async_copy(s, d, sems.at[i]) for i, (s, d) in enumerate(zip(sources, kept))]
    for copy in copies:
        copy.start()
    block = lax.axis_index("seq")
    place = lax.broadcasted_iota(jnp.int32, (VOCAB, VOCAB), 0)
    value = lax.broadcasted_iota(jnp.int32, (VOCAB, VOCAB), 1)
    order = (table_row(value) == place).astype(F32).astype(BF)
    for copy in copies[:5]:
        copy.wait()
    hot_own, hot_prev = hot_columns(ids_ref[...]), hot_columns(prev_ref[...])
    cos_p, sin_p = turn_tables(near_ref, base_ref, slice(0, TOK), block)
    cos_o, sin_o = turn_tables(near_ref, base_ref, slice(TOK, 2 * TOK), block)
    inputs = mm(order, emb[...])
    recip = lax.rsqrt(jnp.mean(inputs * inputs, axis=-1, keepdims=True) + EPSILON)
    normed = (inputs * recip * gain_ref[...]).astype(BF)

    def fill(weight):
        full = mm(normed, weight[...])
        high = full.astype(BF)
        tab[:VOCAB, :] = high
        tab[VOCAB:, :] = (full - high.astype(F32)).astype(BF)

    def gather(hot, cosine, sine, out_ref):
        full = mm_tn(jnp.concatenate([hot, hot], axis=0), tab[...])
        for h in range(HEADS):
            out_ref[:, head(h)] = turn(full[:, head(h)], cosine, sine).astype(BF)

    copies[5].wait()
    fill(wk)
    gather(hot_own, cos_o, sin_o, k_ref)
    gather(hot_prev, cos_p, sin_p, kprev)
    copies[6].wait()
    vtab[...] = mm(normed, wv[...]).astype(BF)
    v_ref[...] = mm_tn(hot_own, vtab[...]).astype(BF)
    vprev[...] = mm_tn(hot_prev, vtab[...]).astype(BF)
    copies[7].wait()
    fill(wq)
    gather(hot_own, cos_o, sin_o, q_ref)
    copies[8].wait()
    copies[9].wait()
    ga_ref[...] = mm(do[...], wo[...]).astype(BF)
    lead = jnp.where(block == 0, NEGATIVE, 0.0).astype(F32)
    scale = HEAD_DIM ** (-0.5)
    own = lax.broadcasted_iota(jnp.int32, (TOK, TOK), 0) <= lax.broadcasted_iota(
        jnp.int32, (TOK, TOK), 1
    )
    for h in range(HEADS):
        query, grad = q_ref[:, head(h)], ga_ref[:, head(h)]
        key_o, key_p = k_ref[:, head(h)], kprev[:, head(h)]
        value_o, value_p = v_ref[:, head(h)], vprev[:, head(h)]
        scores = jnp.where(own, mm_nt(key_o, query), mm_nt(key_p, query) + lead)
        highest = jnp.max(scores, axis=0, keepdims=True)
        weights = jnp.exp((scores - highest) * scale)
        probs = weights * (1.0 / jnp.sum(weights, axis=0, keepdims=True))
        grad_probs = jnp.where(own, mm_nt(value_o, grad), mm_nt(value_p, grad))
        delta = jnp.sum(probs * grad_probs, axis=0, keepdims=True)
        grad_scores = probs * (grad_probs - delta) * scale
        probs_o = jnp.where(own, probs, 0.0).astype(BF)
        probs_p = jnp.where(own, 0.0, probs).astype(BF)
        gs_o = jnp.where(own, grad_scores, 0.0).astype(BF)
        gs_p = jnp.where(own, 0.0, grad_scores).astype(BF)
        vg[:TOK, head(h)] = mm(probs_p, grad).astype(BF)
        vg[TOK:, head(h)] = mm(probs_o, grad).astype(BF)
        kg[:TOK, head(h)] = turn_back(mm(gs_p, query), cos_p, sin_p).astype(BF)
        kg[TOK:, head(h)] = turn_back(mm(gs_o, query), cos_o, sin_o).astype(BF)
        grad_q = mm_tn(gs_o, key_o) + mm_tn(gs_p, key_p)
        gq[:, head(h)] = turn_back(grad_q, cos_o, sin_o).astype(BF)
    hot2 = jnp.concatenate([hot_prev, hot_own], axis=1)
    key_table = mm(hot2, kg[...]).astype(BF)
    out_ref[:, :, :D] = key_table.reshape(PLANE, RING, D)
    value_table = mm(hot2, vg[...]).astype(BF)
    query_table = mm(hot_own, gq[...]).astype(BF)
    grad_normed = mm_nt(key_table, wk[...]) + mm_nt(value_table, wv[...]) + mm_nt(query_table, wq[...])
    out_ref[:, :, D : 2 * D] = grad_normed.astype(BF).reshape(PLANE, RING, D)


def rows_kernel(emb_ref, gain_ref, pick_ref, row_ref, scaled_ref, rows):
    block, lane = lax.axis_index("seq"), lax.axis_index("dp")
    ring = lax.rem(block, RING)
    index = lax.broadcasted_iota(jnp.int32, (RING, VOCAB), 0)
    value = lax.broadcasted_iota(jnp.int32, (RING, VOCAB), 1)
    mine = value == (block - ring + index) * N + lane
    rows[...] = mm(mine.astype(F32).astype(BF), emb_ref[...])
    inputs = rows[...]
    recip = lax.rsqrt(jnp.mean(inputs * inputs, axis=-1, keepdims=True) + EPSILON)
    scaled_ref[...] = inputs * recip
    normed = (scaled_ref[...] * gain_ref[...]).astype(BF)
    place = lax.broadcasted_iota(jnp.int32, (D, 256), 1)
    member = place >> 3
    column = ((member >> 4) << 9) + ring * 64 + ((member & 15) << 2) + (place & 3)
    choose = (lax.broadcasted_iota(jnp.int32, (D, 256), 0) == column).astype(F32).astype(BF)
    picked = mm(normed, choose)
    pick_ref[...] = jnp.concatenate([picked, picked], axis=0).astype(BF)
    row_ref[...] = rows[pl.ds(ring, 1), :]


def share(keep_ref, send_ref):
    high, low = split(keep_ref[:, 2 * D : 2 * D + 128] + keep_ref[:, 2 * D + 128 :])
    keep_ref[:, 2 * D : 2 * D + 128] = high
    keep_ref[:, 2 * D + 128 :] = low
    send_ref[...] = keep_ref[...].astype(BF)


def first_kernel(got_ref, scaled_ref, keep_ref, send_ref, terms):
    total = jnp.sum(got_ref[...].astype(F32), axis=0)
    keep_ref[:, : 2 * D] = total
    product = jnp.sum(total[:, D:] * scaled_ref[...], axis=0, keepdims=True)
    keep_ref[:, 2 * D : 2 * D + 128] = tiles(product, terms)
    keep_ref[:, 2 * D + 128 :] = jnp.zeros((RING, 128), F32)
    share(keep_ref, send_ref)


def total_of(kept_ref, got, columns):
    total = kept_ref[:, columns]
    for ref in got:
        total = total + ref[:, columns].astype(F32)
    return total


def round_kernel(kept_ref, *refs):
    got, (keep_ref, send_ref) = refs[:-2], refs[-2:]
    keep_ref[...] = total_of(kept_ref, got, slice(None))
    share(keep_ref, send_ref)


def weight_kernel(kept_ref, *refs):
    got, (pick_ref, out_ref) = refs[:-2], refs[-2:]
    both = jnp.concatenate(split(total_of(kept_ref, got, slice(0, D))), axis=0).astype(BF)
    part = mm_tn(pick_ref[...], both)
    first = (lax.broadcasted_iota(jnp.int32, (256, 512), 0) & 4) == 0
    part = jnp.where(first, part[:, :512], part[:, 512:])
    out_ref[:, :, :512] = part.reshape(PLANE, 8, 512).astype(BF)
    terms = total_of(kept_ref, got, slice(2 * D, WIDE))
    terms = terms[:, :128] + terms[:, 128:]
    out_ref[:, :, 512:] = jnp.broadcast_to(terms.astype(BF)[None], (PLANE, 8, 128))


def row_kernel(kept_ref, *refs):
    got, (row_ref, gain_ref, ge_ref, rows) = refs[:-4], refs[-4:]
    rows[...] = total_of(kept_ref, got, slice(D, 2 * D))
    grad_normed = rows[pl.ds(lax.rem(lax.axis_index("seq"), RING), 1), :]
    inputs = row_ref[...]
    recip = lax.rsqrt(jnp.mean(inputs * inputs, axis=-1, keepdims=True) + EPSILON)
    grad_scaled = grad_normed * gain_ref[...]
    inner = jnp.mean(grad_scaled * inputs, axis=-1, keepdims=True)
    ge_ref[...] = recip * grad_scaled - inputs * (recip * recip * recip) * inner


def finish_kernel(got_ref, gk_ref, gg_ref):
    total = jnp.sum(got_ref[...].astype(F32), axis=0)
    gk_ref[:, :512] = total[:4, :512]
    gk_ref[:, 512:] = total[4:, :512]
    start = (lax.axis_index("seq") * N + lax.axis_index("dp")) * 4
    mine = lax.broadcasted_iota(jnp.int32, (8, 128), 0) == start // 128
    row = jnp.sum(jnp.where(mine, total[:, 512:], 0.0), axis=0, keepdims=True)
    gg_ref[...] = pltpu.roll(jnp.broadcast_to(row, (8, 128)), 128 - lax.rem(start, 128), 1)


def call(kernel, outs, ins, scratch=(), flops=0, moved=0, limit=16):
    far_space = pl.BlockSpec(memory_space=pltpu.HBM)
    vmem = pl.BlockSpec(memory_space=pltpu.VMEM)
    return pl.pallas_call(
        kernel,
        out_shape=[jax.ShapeDtypeStruct(shape, kind) for shape, kind in outs],
        in_specs=[far_space if far else vmem for _, far in ins],
        out_specs=[vmem] * len(outs),
        scratch_shapes=list(scratch),
        compiler_params=pltpu.CompilerParams(vmem_limit_bytes=limit * MIB),
        cost_estimate=pl.CostEstimate(flops=flops, bytes_accessed=moved, transcendentals=0),
    )(*[value for value, _ in ins])


def local(byte_ids, embedding, gain, w_query, w_key, w_value, w_out, d_output):
    near_table, base_table = (jnp.asarray(table) for table in angle_tables())
    prev_ids = lax.ppermute(byte_ids, "seq", [(i, i + 1) for i in range(N - 1)])
    gain_row = gain.reshape(1, D)
    mat = pltpu.VMEM((D, D), BF)
    tall = pltpu.VMEM((2 * TOK, D), BF)
    flat = pltpu.VMEM((TOK, D), BF)
    near = lambda *values: [(value, False) for value in values]
    far = lambda *values: [(value, True) for value in values]
    (tables,) = call(
        tables_kernel,
        [((PLANE, RING, 2 * D), BF)],
        near(prev_ids)
        + far(embedding, near_table, base_table, byte_ids, gain_row)
        + far(w_key, w_value, w_query, d_output[0], w_out),
        [
            pltpu.VMEM((2, 2 * TOK, 128), F32),
            pltpu.VMEM((2, N, 128), F32),
            pltpu.VMEM((1, TOK), jnp.int32),
            pltpu.VMEM((1, D), F32),
            *[flat, mat, mat, mat, flat, mat, tall],
            *[flat] * 8,
            *[tall, tall],
            pltpu.SemaphoreType.DMA((10,)),
        ],
        flops=8_000_000_000,
        moved=14_000_000,
        limit=56,
    )
    parts = exchange(tables)
    embedding_later, _ = lax.optimization_barrier((embedding, tables))
    pick, row, scaled = call(
        rows_kernel,
        [((16, 256), BF), ((1, D), F32), ((RING, D), F32)],
        near(embedding_later, gain_row),
        [pltpu.VMEM((RING, D), F32)],
        flops=10_000_000,
        moved=600_000,
    )
    both = [((RING, WIDE), F32), ((RING, WIDE), BF)]
    kept, sent = call(
        first_kernel,
        both,
        near(parts, scaled),
        [pltpu.VMEM((8, 128), F32)],
        flops=1_000_000,
        moved=1_300_000,
    )
    for steps in ROUNDS[:-1]:
        got = [swap(sent, step) for step in steps]
        kept, sent = call(round_kernel, both, near(kept, *got), flops=1_000_000, moved=600_000)
    got = [swap(sent, step) for step in ROUNDS[-1]]
    (part,) = call(
        weight_kernel, [((PLANE, 8, 640), BF)], near(kept, *got, pick), flops=10_000_000, moved=400_000
    )
    parts = exchange(part)
    (grad_row,) = call(
        row_kernel,
        [((1, D), F32)],
        near(kept, *got, row, gain_row),
        [pltpu.VMEM((RING, D), F32)],
        flops=1_000_000,
        moved=300_000,
    )
    grad_weight, gain_own = call(
        finish_kernel,
        [((4, D), F32), ((8, 128), F32)],
        near(parts),
        flops=1_000_000,
        moved=200_000,
    )
    return grad_weight, gain_own[0, :4], grad_row


def solution(mesh):
    in_specs = (P("dp", "seq"), P(), P(), P(), P(), P(), P(), P("dp", "seq", None))
    out_specs = (P(("seq", "dp"), None), P(("seq", "dp")), P(("seq", "dp"), None))
    return jax.shard_map(local, mesh=mesh, in_specs=in_specs, out_specs=out_specs, check_vma=False)
```

```python
import functools

import jax
import jax.numpy as jnp
import numpy as np
from jax import lax
from jax.experimental import pallas as pl
from jax.experimental.pallas import tpu as pltpu
from jax.sharding import PartitionSpec as P

HEADS = 8
HEAD_DIM = 128
D = 1024
VOCAB = 256
TOK = 256
N = 16
NEGATIVE = -1e30
EPSILON = 1e-05
THETA = 10000.0
BF = jnp.bfloat16
F32 = jnp.float32
MIB = 1024 * 1024

WIDE = 2 * D + 128
KEYS = D + 128
ROUNDS = ((1, 4, 4, 256), (8, 2, 2, 128), (4, 2, 1, 128))


def exchange(value, axis):
    return lax.all_to_all(value, axis, 0, 0, tiled=False)


def swap(value, step):
    return lax.ppermute(value, "seq", [(i, i ^ step) for i in range(N)])


def angle_tables():
    inverse = THETA ** (-np.arange(HEAD_DIM // 2, dtype=np.float64) / (HEAD_DIM // 2))
    near = np.arange(-TOK, TOK, dtype=np.float64)[:, None] * inverse[None, :]
    base = (TOK * np.arange(16, dtype=np.float64))[:, None] * inverse[None, :]

    def wide(angle):
        cosine, sine = np.cos(angle), np.sin(angle)
        return np.stack(
            [np.concatenate([cosine, cosine], -1), np.concatenate([-sine, sine], -1)]
        ).astype(np.float32)

    return wide(near), wide(base)


def mm(left, right):
    return lax.dot_general(left, right, (((1,), (0,)), ((), ())), preferred_element_type=F32)


def mm_nt(left, right):
    return lax.dot_general(left, right, (((1,), (1,)), ((), ())), preferred_element_type=F32)


def mm_tn(left, right):
    return lax.dot_general(left, right, (((0,), (0,)), ((), ())), preferred_element_type=F32)


def table_row(ids):
    return ((ids & 15) << 4) | (((ids >> 4) & 3) << 2) | (ids >> 6)


def hot_columns(ids_row):
    place = lax.broadcasted_iota(jnp.int32, (VOCAB, TOK), 0)
    return (place == table_row(ids_row)).astype(F32).astype(BF)


def turn_tables(near_ref, base_ref, rows, block):
    near_c, near_s = near_ref[0, rows, :], near_ref[1, rows, :]
    base_c, base_s = base_ref[0, pl.ds(block, 1), :], base_ref[1, pl.ds(block, 1), :]
    return near_c * base_c - near_s * base_s, near_s * base_c + near_c * base_s


def turn(value, cosine, sine):
    return value * cosine + pltpu.roll(value, HEAD_DIM // 2, 1) * sine


def turn_back(value, cosine, sine):
    return value * cosine - pltpu.roll(value, HEAD_DIM // 2, 1) * sine


def head(index):
    return slice(index * HEAD_DIM, (index + 1) * HEAD_DIM)


def split(value):
    high = value.astype(BF).astype(F32)
    return high, value - high


def tiles(value, scratch):
    for k in range(8):
        scratch[k : k + 1, :] = value[:, k * 128 : (k + 1) * 128]
    return scratch[...]


def halve(value, step, count, keep_ref, send_ref):
    bit = (lax.axis_index("seq") // step) % 2
    keep_ref[...] = value[pl.ds(pl.multiple_of(bit * count, count), count), :]
    send_ref[...] = value[pl.ds(pl.multiple_of((1 - bit) * count, count), count), :].astype(BF)


def tables_kernel(*refs):
    prev_ref, sources, (out_ref,) = refs[0], refs[1:11], refs[11:12]
    near_ref, base_ref, ids_ref, gain_ref, emb, wk, wv, wq, do, wo = refs[12:22]
    tab, q_ref, k_ref, v_ref, ga_ref, kprev, vprev, vtab, gq, kg, vg, scaled, terms, sems = refs[22:]
    kept = (emb, near_ref, base_ref, ids_ref, gain_ref, wk, wv, wq, do, wo)
    copies = [pltpu.make_async_copy(s, d, sems.at[i]) for i, (s, d) in enumerate(zip(sources, kept))]
    for copy in copies:
        copy.start()
    block = lax.axis_index("seq")
    place = lax.broadcasted_iota(jnp.int32, (VOCAB, VOCAB), 0)
    value = lax.broadcasted_iota(jnp.int32, (VOCAB, VOCAB), 1)
    order = (table_row(value) == place).astype(F32).astype(BF)
    for copy in copies[:5]:
        copy.wait()
    hot_own, hot_prev = hot_columns(ids_ref[...]), hot_columns(prev_ref[...])
    rows_own, rows_prev = hot_own.T, hot_prev.T
    cos_p, sin_p = turn_tables(near_ref, base_ref, slice(0, TOK), block)
    cos_o, sin_o = turn_tables(near_ref, base_ref, slice(TOK, 2 * TOK), block)
    inputs = mm(order, emb[...])
    recip = lax.rsqrt(jnp.mean(inputs * inputs, axis=-1, keepdims=True) + EPSILON)
    scaled[...] = inputs * recip
    normed = (scaled[...] * gain_ref[...]).astype(BF)

    def fill(weight):
        full = mm(normed, weight[...])
        high = full.astype(BF)
        tab[:VOCAB, :] = high
        tab[VOCAB:, :] = (full - high.astype(F32)).astype(BF)

    def gather(hot, cosine, sine, out_ref):
        full = mm(jnp.concatenate([hot, hot], axis=1), tab[...])
        for h in range(HEADS):
            out_ref[:, head(h)] = turn(full[:, head(h)], cosine, sine).astype(BF)

    copies[5].wait()
    fill(wk)
    gather(rows_own, cos_o, sin_o, k_ref)
    gather(rows_prev, cos_p, sin_p, kprev)
    copies[6].wait()
    vtab[...] = mm(normed, wv[...]).astype(BF)
    v_ref[...] = mm(rows_own, vtab[...]).astype(BF)
    vprev[...] = mm(rows_prev, vtab[...]).astype(BF)
    copies[7].wait()
    fill(wq)
    gather(rows_own, cos_o, sin_o, q_ref)
    copies[8].wait()
    copies[9].wait()
    ga_ref[...] = mm(do[...], wo[...]).astype(BF)
    lead = jnp.where(block == 0, NEGATIVE, 0.0).astype(F32)
    scale = HEAD_DIM ** (-0.5)
    own = lax.broadcasted_iota(jnp.int32, (TOK, TOK), 0) <= lax.broadcasted_iota(
        jnp.int32, (TOK, TOK), 1
    )
    behind_o = own.astype(F32).T.astype(BF)
    behind_p = 1 - behind_o
    for h in range(HEADS):
        query, grad = q_ref[:, head(h)], ga_ref[:, head(h)]
        key_o, key_p = k_ref[:, head(h)], kprev[:, head(h)]
        value_o, value_p = v_ref[:, head(h)], vprev[:, head(h)]
        scores = jnp.where(own, mm_nt(key_o, query), mm_nt(key_p, query) + lead)
        highest = jnp.max(scores, axis=0, keepdims=True)
        weights = jnp.exp((scores - highest) * scale)
        probs = weights * (1.0 / jnp.sum(weights, axis=0, keepdims=True))
        grad_probs = jnp.where(own, mm_nt(value_o, grad), mm_nt(value_p, grad))
        delta = jnp.sum(probs * grad_probs, axis=0, keepdims=True)
        grad_scores = probs * (grad_probs - delta) * scale
        probs_o = jnp.where(own, probs, 0.0).astype(BF)
        probs_p = jnp.where(own, 0.0, probs).astype(BF)
        gs_o = jnp.where(own, grad_scores, 0.0).astype(BF)
        gs_p = jnp.where(own, 0.0, grad_scores).astype(BF)
        turned = grad_scores.astype(BF).T
        vg[:TOK, head(h)] = mm(probs_p, grad).astype(BF)
        vg[TOK:, head(h)] = mm(probs_o, grad).astype(BF)
        kg[:TOK, head(h)] = turn_back(mm(gs_p, query), cos_p, sin_p).astype(BF)
        kg[TOK:, head(h)] = turn_back(mm(gs_o, query), cos_o, sin_o).astype(BF)
        grad_q = mm(turned * behind_o, key_o) + mm(turned * behind_p, key_p)
        gq[:, head(h)] = turn_back(grad_q, cos_o, sin_o).astype(BF)
    hot2 = jnp.concatenate([hot_prev, hot_own], axis=1)
    key_table = mm(hot2, kg[...]).astype(BF)
    out_ref[:, :, :D] = key_table.reshape(N, N, D)
    value_table = mm(hot2, vg[...]).astype(BF)
    query_table = mm(hot_own, gq[...]).astype(BF)
    grad_normed = mm_nt(key_table, wk[...]) + mm_nt(value_table, wv[...]) + mm_nt(query_table, wq[...])
    out_ref[:, :, D : 2 * D] = grad_normed.astype(BF).reshape(N, N, D)
    product = jnp.sum(grad_normed * scaled[...], axis=0, keepdims=True)
    gain_terms = jnp.concatenate(split(tiles(product, terms)), axis=0).astype(BF)
    out_ref[:, :, 2 * D :] = jnp.broadcast_to(gain_terms[None], (N, N, 128))


def rows_kernel(emb_ref, gain_ref, pick_ref, row_ref):
    block, lane = lax.axis_index("seq"), lax.axis_index("dp")
    index = lax.broadcasted_iota(jnp.int32, (2 * N, VOCAB), 0)
    value = lax.broadcasted_iota(jnp.int32, (2 * N, VOCAB), 1)
    wanted = jnp.where(index < N, N * lane + index, table_row(N * block + lane))
    inputs = mm((table_row(value) == wanted).astype(F32).astype(BF), emb_ref[...])
    recip = lax.rsqrt(jnp.mean(inputs * inputs, axis=-1, keepdims=True) + EPSILON)
    normed = (inputs * recip * gain_ref[...]).astype(BF)
    place = lax.broadcasted_iota(jnp.int32, (D, 128), 1)
    column = block * 64 + ((place >> 3) << 2) + (place & 3)
    choose = (lax.broadcasted_iota(jnp.int32, (D, 128), 0) == column).astype(F32).astype(BF)
    picked = mm(normed, choose)[:N]
    pick_ref[...] = jnp.concatenate([picked, picked], axis=0).astype(BF)
    row_ref[...] = inputs[N : N + 1]


def pack(rows, width):
    parts = [rows[:, k : k + width] for k in range(0, D, width)]
    if len(parts) * rows.shape[0] < N:
        parts.append(jnp.zeros((N - len(parts) * rows.shape[0], width), F32))
    return jnp.concatenate(parts, axis=0)


def unpack(packed, count, width):
    return jnp.concatenate([packed[k * count : (k + 1) * count] for k in range(D // width)], axis=1)


def share(keys_ref, grads, turn_of, kept_ref, sends):
    unit, ways, count, width = turn_of
    high, low = split(keys_ref[:8, D:] + keys_ref[8:, D:])
    keys_ref[:8, D:] = high
    keys_ref[8:, D:] = low
    place = (lax.axis_index("seq") // unit) % ways
    parts = [grads[k * count : (k + 1) * count] for k in range(ways)]

    def part(index):
        chosen = parts[0]
        for k in range(1, ways):
            chosen = jnp.where(index == k, parts[k], chosen)
        return chosen

    kept_ref[...] = part(place)
    keys = keys_ref[...].astype(BF)
    for k, send_ref in enumerate(sends):
        send_ref[:, :KEYS] = keys
        send_ref[:, KEYS:] = pack(part(place ^ (k + 1)), width).astype(BF)


def first_kernel(got_ref, keys_ref, kept_ref, *sends):
    total = jnp.sum(got_ref[...].astype(F32), axis=0)
    keys_ref[:, :D] = total[:, :D]
    keys_ref[:, D:] = total[:, 2 * D :]
    share(keys_ref, total[:, D : 2 * D], ROUNDS[0], kept_ref, sends)


def key_sum(keys_ref, got, columns):
    return sum((ref[:, columns].astype(F32) for ref in got), keys_ref[:, columns])


def grad_sum(kept_ref, got, turn_of):
    return sum((unpack(ref[:, KEYS:].astype(F32), *turn_of[2:]) for ref in got), kept_ref[...])


def round_kernel(index, old_ref, kept_ref, *refs):
    others = ROUNDS[index][1] - 1
    got, keys_ref, next_ref, sends = refs[:others], refs[others], refs[others + 1], refs[others + 2 :]
    keys_ref[...] = key_sum(old_ref, got, slice(0, KEYS))
    share(keys_ref, grad_sum(kept_ref, got, ROUNDS[index]), ROUNDS[index + 1], next_ref, sends)


def weight_kernel(keys_ref, *refs):
    got, (pick_ref, out_ref) = refs[:-2], refs[-2:]
    both = jnp.concatenate(split(key_sum(keys_ref, got, slice(0, D))), axis=0).astype(BF)
    part = mm_tn(pick_ref[...], both)
    first = (lax.broadcasted_iota(jnp.int32, (128, 512), 0) & 4) == 0
    out_ref[...] = jnp.where(first, part[:, :512], part[:, 512:]).reshape(N, 8, 512).astype(BF)


def row_kernel(keys_ref, kept_ref, *refs):
    got, (row_ref, gain_ref, ge_ref, gg_ref, sums) = refs[:-5], refs[-5:]
    sums[...] = key_sum(keys_ref, got, slice(D, KEYS))
    grad_normed = grad_sum(kept_ref, got, ROUNDS[-1])
    inputs = row_ref[...]
    recip = lax.rsqrt(jnp.mean(inputs * inputs, axis=-1, keepdims=True) + EPSILON)
    grad_scaled = grad_normed * gain_ref[...]
    inner = jnp.mean(grad_scaled * inputs, axis=-1, keepdims=True)
    ge_ref[...] = recip * grad_scaled - inputs * (recip * recip * recip) * inner
    terms = sums[:8] + sums[8:]
    start = (lax.axis_index("seq") * N + lax.axis_index("dp")) * 4
    mine = lax.broadcasted_iota(jnp.int32, (8, 128), 0) == start // 128
    row = jnp.sum(jnp.where(mine, terms, 0.0), axis=0, keepdims=True)
    gg_ref[...] = pltpu.roll(jnp.broadcast_to(row, (8, 128)), 128 - lax.rem(start, 128), 1)


def finish_kernel(got_ref, gk_ref):
    total = jnp.sum(got_ref[...].astype(F32), axis=0)
    gk_ref[:, :512] = total[:4]
    gk_ref[:, 512:] = total[4:]


def call(kernel, outs, ins, scratch=(), flops=0, moved=0, limit=16):
    far_space = pl.BlockSpec(memory_space=pltpu.HBM)
    vmem = pl.BlockSpec(memory_space=pltpu.VMEM)
    return pl.pallas_call(
        kernel,
        out_shape=[jax.ShapeDtypeStruct(shape, kind) for shape, kind in outs],
        in_specs=[far_space if far else vmem for _, far in ins],
        out_specs=[vmem] * len(outs),
        scratch_shapes=list(scratch),
        compiler_params=pltpu.CompilerParams(vmem_limit_bytes=limit * MIB),
        cost_estimate=pl.CostEstimate(flops=flops, bytes_accessed=moved, transcendentals=0),
    )(*[value for value, _ in ins])


def local(byte_ids, embedding, gain, w_query, w_key, w_value, w_out, d_output):
    near_table, base_table = (jnp.asarray(table) for table in angle_tables())
    prev_ids = lax.ppermute(byte_ids, "seq", [(i, i + 1) for i in range(N - 1)])
    gain_row = gain.reshape(1, D)
    mat = pltpu.VMEM((D, D), BF)
    tall = pltpu.VMEM((2 * TOK, D), BF)
    flat = pltpu.VMEM((TOK, D), BF)
    near = lambda *values: [(value, False) for value in values]
    far = lambda *values: [(value, True) for value in values]
    (tables,) = call(
        tables_kernel,
        [((N, N, WIDE), BF)],
        near(prev_ids)
        + far(embedding, near_table, base_table, byte_ids, gain_row)
        + far(w_key, w_value, w_query, d_output[0], w_out),
        [
            pltpu.VMEM((2, 2 * TOK, 128), F32),
            pltpu.VMEM((2, N, 128), F32),
            pltpu.VMEM((1, TOK), jnp.int32),
            pltpu.VMEM((1, D), F32),
            *[flat, mat, mat, mat, flat, mat, tall],
            *[flat] * 8,
            *[tall, tall],
            pltpu.VMEM((VOCAB, D), F32),
            pltpu.VMEM((8, 128), F32),
            pltpu.SemaphoreType.DMA((10,)),
        ],
        flops=8_000_000_000,
        moved=14_000_000,
        limit=56,
    )
    parts = exchange(tables, "dp")
    embedding_later, _ = lax.optimization_barrier((embedding, tables))
    pick, row = call(
        rows_kernel,
        [((32, 128), BF), ((1, D), F32)],
        near(embedding_later, gain_row),
        flops=10_000_000,
        moved=600_000,
    )
    def held(unit, ways, count, width):
        return [((N, KEYS), F32), ((count, D), F32)] + [((N, KEYS + width), BF)] * (ways - 1)

    def spread(sends, unit):
        return [swap(value, unit * (k + 1)) for k, value in enumerate(sends)]

    keys, kept, *sends = call(
        first_kernel, held(*ROUNDS[0]), near(parts), flops=1_000_000, moved=1_300_000
    )
    for index in range(len(ROUNDS) - 1):
        keys, kept, *sends = call(
            functools.partial(round_kernel, index),
            held(*ROUNDS[index + 1]),
            near(keys, kept, *spread(sends, ROUNDS[index][0])),
            flops=1_000_000,
            moved=400_000,
        )
    got = spread(sends, ROUNDS[-1][0])
    (part,) = call(
        weight_kernel, [((N, 8, 512), BF)], near(keys, *got, pick), flops=10_000_000, moved=400_000
    )
    parts = exchange(part, "dp")
    grad_row, gain_own = call(
        row_kernel,
        [((1, D), F32), ((8, 128), F32)],
        near(keys, kept, *got, row, gain_row),
        [pltpu.VMEM((N, 128), F32)],
        flops=1_000_000,
        moved=200_000,
    )
    (grad_weight,) = call(finish_kernel, [((4, D), F32)], near(parts), flops=1_000_000, moved=200_000)
    return grad_weight, gain_own[0, :4], grad_row


def solution(mesh):
    in_specs = (P("dp", "seq"), P(), P(), P(), P(), P(), P(), P("dp", "seq", None))
    out_specs = (P(("seq", "dp"), None), P(("seq", "dp")), P(("seq", "dp"), None))
    return jax.shard_map(local, mesh=mesh, in_specs=in_specs, out_specs=out_specs, check_vma=False)
```

```python
import functools

import jax
import jax.numpy as jnp
import numpy as np
from jax import lax
from jax.experimental import pallas as pl
from jax.experimental.pallas import tpu as pltpu
from jax.sharding import PartitionSpec as P

HEADS = 8
HEAD_DIM = 128
D = 1024
VOCAB = 256
TOK = 256
N = 16
NEGATIVE = -1e30
EPSILON = 1e-05
THETA = 10000.0
BF = jnp.bfloat16
F32 = jnp.float32
MIB = 1024 * 1024

WIDE = 2 * D + 128
KEYS = D + 128
ROUNDS = ((1, 4, 4, 256), (8, 2, 2, 128), (4, 2, 1, 128))


def exchange(value, axis):
    return lax.all_to_all(value, axis, 0, 0, tiled=False)


def swap(value, step):
    return lax.ppermute(value, "seq", [(i, i ^ step) for i in range(N)])


def angle_tables():
    inverse = THETA ** (-np.arange(HEAD_DIM // 2, dtype=np.float64) / (HEAD_DIM // 2))
    near = np.arange(-TOK, TOK, dtype=np.float64)[:, None] * inverse[None, :]
    base = (TOK * np.arange(16, dtype=np.float64))[:, None] * inverse[None, :]

    def wide(angle):
        cosine, sine = np.cos(angle), np.sin(angle)
        return np.stack(
            [np.concatenate([cosine, cosine], -1), np.concatenate([-sine, sine], -1)]
        ).astype(np.float32)

    return wide(near), wide(base)


def mm(left, right):
    return lax.dot_general(left, right, (((1,), (0,)), ((), ())), preferred_element_type=F32)


def mm_nt(left, right):
    return lax.dot_general(left, right, (((1,), (1,)), ((), ())), preferred_element_type=F32)


def mm_tn(left, right):
    return lax.dot_general(left, right, (((0,), (0,)), ((), ())), preferred_element_type=F32)


def table_row(ids):
    return ((ids & 15) << 4) | (((ids >> 4) & 3) << 2) | (ids >> 6)


def hot_columns(ids_row):
    place = lax.broadcasted_iota(jnp.int32, (VOCAB, TOK), 0)
    return (place == table_row(ids_row)).astype(F32).astype(BF)


def turn_tables(near_ref, base_ref, rows, block):
    near_c, near_s = near_ref[0, rows, :], near_ref[1, rows, :]
    base_c, base_s = base_ref[0, pl.ds(block, 1), :], base_ref[1, pl.ds(block, 1), :]
    return near_c * base_c - near_s * base_s, near_s * base_c + near_c * base_s


def turn(value, cosine, sine):
    return value * cosine + pltpu.roll(value, HEAD_DIM // 2, 1) * sine


def turn_back(value, cosine, sine):
    return value * cosine - pltpu.roll(value, HEAD_DIM // 2, 1) * sine


def head(index):
    return slice(index * HEAD_DIM, (index + 1) * HEAD_DIM)


def split(value):
    high = value.astype(BF).astype(F32)
    return high, value - high


def tiles(value, scratch):
    for k in range(8):
        scratch[k : k + 1, :] = value[:, k * 128 : (k + 1) * 128]
    return scratch[...]


def halve(value, step, count, keep_ref, send_ref):
    bit = (lax.axis_index("seq") // step) % 2
    keep_ref[...] = value[pl.ds(pl.multiple_of(bit * count, count), count), :]
    send_ref[...] = value[pl.ds(pl.multiple_of((1 - bit) * count, count), count), :].astype(BF)


def tables_kernel(*refs):
    sources, (out_ref,) = refs[:11], refs[11:12]
    prev_ref, near_ref, base_ref, ids_ref, gain_ref, emb, wk, wv, wq, do, wo = refs[12:23]
    tab, q_ref, k_ref, v_ref, ga_ref, kprev, vprev, vtab, gq, kg, vg, scaled, terms, sems = refs[23:]
    kept = (emb, gain_ref, ids_ref, prev_ref, near_ref, base_ref, wk, wv, wq, do, wo)
    copies = [pltpu.make_async_copy(s, d, sems.at[i]) for i, (s, d) in enumerate(zip(sources, kept))]
    for copy in copies[:7]:
        copy.start()
    block = lax.axis_index("seq")
    place = lax.broadcasted_iota(jnp.int32, (VOCAB, VOCAB), 0)
    value = lax.broadcasted_iota(jnp.int32, (VOCAB, VOCAB), 1)
    order = (table_row(value) == place).astype(F32).astype(BF)
    copies[0].wait()
    copies[1].wait()
    copies[7].start()
    copies[8].start()
    inputs = mm(order, emb[...])
    recip = lax.rsqrt(jnp.mean(inputs * inputs, axis=-1, keepdims=True) + EPSILON)
    scaled[...] = inputs * recip
    normed = (scaled[...] * gain_ref[...]).astype(BF)

    for copy in copies[2:6]:
        copy.wait()
    hot_own, hot_prev = hot_columns(ids_ref[...]), hot_columns(prev_ref[...])
    rows_own, rows_prev = hot_own.T, hot_prev.T
    cos_p, sin_p = turn_tables(near_ref, base_ref, slice(0, TOK), block)
    cos_o, sin_o = turn_tables(near_ref, base_ref, slice(TOK, 2 * TOK), block)

    def fill(weight):
        full = mm(normed, weight[...])
        high = full.astype(BF)
        tab[:VOCAB, :] = high
        tab[VOCAB:, :] = (full - high.astype(F32)).astype(BF)

    def gather(hot, cosine, sine, out_ref):
        full = mm(jnp.concatenate([hot, hot], axis=1), tab[...])
        for h in range(HEADS):
            out_ref[:, head(h)] = turn(full[:, head(h)], cosine, sine).astype(BF)

    copies[6].wait()
    copies[9].start()
    copies[10].start()
    fill(wk)
    gather(rows_own, cos_o, sin_o, k_ref)
    gather(rows_prev, cos_p, sin_p, kprev)
    copies[7].wait()
    vtab[...] = mm(normed, wv[...]).astype(BF)
    v_ref[...] = mm(rows_own, vtab[...]).astype(BF)
    vprev[...] = mm(rows_prev, vtab[...]).astype(BF)
    copies[8].wait()
    fill(wq)
    gather(rows_own, cos_o, sin_o, q_ref)
    copies[9].wait()
    copies[10].wait()
    ga_ref[...] = mm(do[...], wo[...]).astype(BF)
    lead = jnp.where(block == 0, NEGATIVE, 0.0).astype(F32)
    scale = HEAD_DIM ** (-0.5)
    own = lax.broadcasted_iota(jnp.int32, (TOK, TOK), 0) <= lax.broadcasted_iota(
        jnp.int32, (TOK, TOK), 1
    )
    behind_o = own.astype(F32).T.astype(BF)
    behind_p = 1 - behind_o
    for h in range(HEADS):
        query, grad = q_ref[:, head(h)], ga_ref[:, head(h)]
        key_o, key_p = k_ref[:, head(h)], kprev[:, head(h)]
        value_o, value_p = v_ref[:, head(h)], vprev[:, head(h)]
        scores = jnp.where(own, mm_nt(key_o, query), mm_nt(key_p, query) + lead)
        highest = jnp.max(scores, axis=0, keepdims=True)
        weights = jnp.exp((scores - highest) * scale)
        probs = weights * (1.0 / jnp.sum(weights, axis=0, keepdims=True))
        grad_probs = jnp.where(own, mm_nt(value_o, grad), mm_nt(value_p, grad))
        delta = jnp.sum(probs * grad_probs, axis=0, keepdims=True)
        grad_scores = probs * (grad_probs - delta) * scale
        probs_o = jnp.where(own, probs, 0.0).astype(BF)
        probs_p = jnp.where(own, 0.0, probs).astype(BF)
        gs_o = jnp.where(own, grad_scores, 0.0).astype(BF)
        gs_p = jnp.where(own, 0.0, grad_scores).astype(BF)
        turned = grad_scores.astype(BF).T
        vg[:TOK, head(h)] = mm(probs_p, grad).astype(BF)
        vg[TOK:, head(h)] = mm(probs_o, grad).astype(BF)
        kg[:TOK, head(h)] = turn_back(mm(gs_p, query), cos_p, sin_p).astype(BF)
        kg[TOK:, head(h)] = turn_back(mm(gs_o, query), cos_o, sin_o).astype(BF)
        grad_q = mm(turned * behind_o, key_o) + mm(turned * behind_p, key_p)
        gq[:, head(h)] = turn_back(grad_q, cos_o, sin_o).astype(BF)
    hot2 = jnp.concatenate([hot_prev, hot_own], axis=1)
    key_table = mm(hot2, kg[...]).astype(BF)
    out_ref[:, :, :D] = key_table.reshape(N, N, D)
    value_table = mm(hot2, vg[...]).astype(BF)
    query_table = mm(hot_own, gq[...]).astype(BF)
    grad_normed = mm_nt(key_table, wk[...]) + mm_nt(value_table, wv[...]) + mm_nt(query_table, wq[...])
    out_ref[:, :, D : 2 * D] = grad_normed.astype(BF).reshape(N, N, D)
    product = jnp.sum(grad_normed * scaled[...], axis=0, keepdims=True)
    gain_terms = jnp.concatenate(split(tiles(product, terms)), axis=0).astype(BF)
    out_ref[:, :, 2 * D :] = jnp.broadcast_to(gain_terms[None], (N, N, 128))


def rows_kernel(emb_ref, gain_ref, pick_ref, row_ref):
    block, lane = lax.axis_index("seq"), lax.axis_index("dp")
    index = lax.broadcasted_iota(jnp.int32, (2 * N, VOCAB), 0)
    value = lax.broadcasted_iota(jnp.int32, (2 * N, VOCAB), 1)
    wanted = jnp.where(index < N, N * lane + index, table_row(N * block + lane))
    inputs = mm((table_row(value) == wanted).astype(F32).astype(BF), emb_ref[...])
    recip = lax.rsqrt(jnp.mean(inputs * inputs, axis=-1, keepdims=True) + EPSILON)
    normed = (inputs * recip * gain_ref[...]).astype(BF)
    place = lax.broadcasted_iota(jnp.int32, (D, 128), 1)
    column = block * 64 + ((place >> 3) << 2) + (place & 3)
    choose = (lax.broadcasted_iota(jnp.int32, (D, 128), 0) == column).astype(F32).astype(BF)
    picked = mm(normed, choose)[:N]
    pick_ref[...] = jnp.concatenate([picked, picked], axis=0).astype(BF)
    row_ref[...] = inputs[N : N + 1]


def pack(rows, width):
    parts = [rows[:, k : k + width] for k in range(0, D, width)]
    if len(parts) * rows.shape[0] < N:
        parts.append(jnp.zeros((N - len(parts) * rows.shape[0], width), F32))
    return jnp.concatenate(parts, axis=0)


def unpack(packed, count, width):
    return jnp.concatenate([packed[k * count : (k + 1) * count] for k in range(D // width)], axis=1)


def share(keys_ref, grads, turn_of, kept_ref, sends):
    unit, ways, count, width = turn_of
    high, low = split(keys_ref[:8, D:] + keys_ref[8:, D:])
    keys_ref[:8, D:] = high
    keys_ref[8:, D:] = low
    place = (lax.axis_index("seq") // unit) % ways
    parts = [grads[k * count : (k + 1) * count] for k in range(ways)]

    def part(index):
        chosen = parts[0]
        for k in range(1, ways):
            chosen = jnp.where(index == k, parts[k], chosen)
        return chosen

    kept_ref[...] = part(place)
    keys = keys_ref[...].astype(BF)
    for k, send_ref in enumerate(sends):
        send_ref[:, :KEYS] = keys
        send_ref[:, KEYS:] = pack(part(place ^ (k + 1)), width).astype(BF)


def first_kernel(got_ref, keys_ref, kept_ref, *sends):
    total = jnp.sum(got_ref[...].astype(F32), axis=0)
    keys_ref[:, :D] = total[:, :D]
    keys_ref[:, D:] = total[:, 2 * D :]
    share(keys_ref, total[:, D : 2 * D], ROUNDS[0], kept_ref, sends)


def key_sum(keys_ref, got, columns):
    return sum((ref[:, columns].astype(F32) for ref in got), keys_ref[:, columns])


def grad_sum(kept_ref, got, turn_of):
    return sum((unpack(ref[:, KEYS:].astype(F32), *turn_of[2:]) for ref in got), kept_ref[...])


def round_kernel(index, old_ref, kept_ref, *refs):
    others = ROUNDS[index][1] - 1
    got, keys_ref, next_ref, sends = refs[:others], refs[others], refs[others + 1], refs[others + 2 :]
    keys_ref[...] = key_sum(old_ref, got, slice(0, KEYS))
    share(keys_ref, grad_sum(kept_ref, got, ROUNDS[index]), ROUNDS[index + 1], next_ref, sends)


def weight_kernel(keys_ref, *refs):
    got, (pick_ref, out_ref) = refs[:-2], refs[-2:]
    both = jnp.concatenate(split(key_sum(keys_ref, got, slice(0, D))), axis=0).astype(BF)
    part = mm_tn(pick_ref[...], both)
    first = (lax.broadcasted_iota(jnp.int32, (128, 512), 0) & 4) == 0
    out_ref[...] = jnp.where(first, part[:, :512], part[:, 512:]).reshape(N, 8, 512).astype(BF)


def row_kernel(keys_ref, kept_ref, *refs):
    got, (row_ref, gain_ref, ge_ref, gg_ref, sums) = refs[:-5], refs[-5:]
    sums[...] = key_sum(keys_ref, got, slice(D, KEYS))
    grad_normed = grad_sum(kept_ref, got, ROUNDS[-1])
    inputs = row_ref[...]
    recip = lax.rsqrt(jnp.mean(inputs * inputs, axis=-1, keepdims=True) + EPSILON)
    grad_scaled = grad_normed * gain_ref[...]
    inner = jnp.mean(grad_scaled * inputs, axis=-1, keepdims=True)
    ge_ref[...] = recip * grad_scaled - inputs * (recip * recip * recip) * inner
    terms = sums[:8] + sums[8:]
    start = (lax.axis_index("seq") * N + lax.axis_index("dp")) * 4
    mine = lax.broadcasted_iota(jnp.int32, (8, 128), 0) == start // 128
    row = jnp.sum(jnp.where(mine, terms, 0.0), axis=0, keepdims=True)
    gg_ref[...] = pltpu.roll(jnp.broadcast_to(row, (8, 128)), 128 - lax.rem(start, 128), 1)


def finish_kernel(got_ref, gk_ref):
    total = jnp.sum(got_ref[...].astype(F32), axis=0)
    gk_ref[:, :512] = total[:4]
    gk_ref[:, 512:] = total[4:]


def call(kernel, outs, ins, scratch=(), flops=0, moved=0, limit=16):
    far_space = pl.BlockSpec(memory_space=pl.ANY)
    vmem = pl.BlockSpec(memory_space=pltpu.VMEM)
    return pl.pallas_call(
        kernel,
        out_shape=[jax.ShapeDtypeStruct(shape, kind) for shape, kind in outs],
        in_specs=[far_space if far else vmem for _, far in ins],
        out_specs=[vmem] * len(outs),
        scratch_shapes=list(scratch),
        compiler_params=pltpu.CompilerParams(vmem_limit_bytes=limit * MIB),
        cost_estimate=pl.CostEstimate(flops=flops, bytes_accessed=moved, transcendentals=0),
    )(*[value for value, _ in ins])


def local(byte_ids, embedding, gain, w_query, w_key, w_value, w_out, d_output):
    near_table, base_table = (jnp.asarray(table) for table in angle_tables())
    prev_ids = lax.ppermute(byte_ids, "seq", [(i, i + 1) for i in range(N - 1)])
    gain_row = gain.reshape(1, D)
    mat = pltpu.VMEM((D, D), BF)
    tall = pltpu.VMEM((2 * TOK, D), BF)
    flat = pltpu.VMEM((TOK, D), BF)
    near = lambda *values: [(value, False) for value in values]
    far = lambda *values: [(value, True) for value in values]
    (tables,) = call(
        tables_kernel,
        [((N, N, WIDE), BF)],
        far(embedding, gain_row, byte_ids, prev_ids, near_table, base_table)
        + far(w_key, w_value, w_query, d_output[0], w_out),
        [
            pltpu.VMEM((1, TOK), jnp.int32),
            pltpu.VMEM((2, 2 * TOK, 128), F32),
            pltpu.VMEM((2, N, 128), F32),
            pltpu.VMEM((1, TOK), jnp.int32),
            pltpu.VMEM((1, D), F32),
            *[flat, mat, mat, mat, flat, mat, tall],
            *[flat] * 8,
            *[tall, tall],
            pltpu.VMEM((VOCAB, D), F32),
            pltpu.VMEM((8, 128), F32),
            pltpu.SemaphoreType.DMA((11,)),
        ],
        flops=8_000_000_000,
        moved=14_000_000,
        limit=56,
    )
    parts = exchange(tables, "dp")
    embedding_later, _ = lax.optimization_barrier((embedding, tables))
    pick, row = call(
        rows_kernel,
        [((32, 128), BF), ((1, D), F32)],
        near(embedding_later, gain_row),
        flops=10_000_000,
        moved=600_000,
    )
    def held(unit, ways, count, width):
        return [((N, KEYS), F32), ((count, D), F32)] + [((N, KEYS + width), BF)] * (ways - 1)

    def spread(sends, unit):
        return [swap(value, unit * (k + 1)) for k, value in enumerate(sends)]

    keys, kept, *sends = call(
        first_kernel, held(*ROUNDS[0]), near(parts), flops=1_000_000, moved=1_300_000
    )
    for index in range(len(ROUNDS) - 1):
        keys, kept, *sends = call(
            functools.partial(round_kernel, index),
            held(*ROUNDS[index + 1]),
            near(keys, kept, *spread(sends, ROUNDS[index][0])),
            flops=1_000_000,
            moved=400_000,
        )
    got = spread(sends, ROUNDS[-1][0])
    (part,) = call(
        weight_kernel, [((N, 8, 512), BF)], near(keys, *got, pick), flops=10_000_000, moved=400_000
    )
    parts = exchange(part, "dp")
    grad_row, gain_own = call(
        row_kernel,
        [((1, D), F32), ((8, 128), F32)],
        near(keys, kept, *got, row, gain_row),
        [pltpu.VMEM((N, 128), F32)],
        flops=1_000_000,
        moved=200_000,
    )
    (grad_weight,) = call(finish_kernel, [((4, D), F32)], near(parts), flops=1_000_000, moved=200_000)
    return grad_weight, gain_own[0, :4], grad_row


def solution(mesh):
    in_specs = (P("dp", "seq"), P(), P(), P(), P(), P(), P(), P("dp", "seq", None))
    out_specs = (P(("seq", "dp"), None), P(("seq", "dp")), P(("seq", "dp"), None))
    return jax.shard_map(local, mesh=mesh, in_specs=in_specs, out_specs=out_specs, check_vma=False)
```

```python
import functools

import jax
import jax.numpy as jnp
import numpy as np
from jax import lax
from jax.experimental import pallas as pl
from jax.experimental.pallas import tpu as pltpu
from jax.sharding import PartitionSpec as P

HEADS = 8
HEAD_DIM = 128
D = 1024
VOCAB = 256
TOK = 256
N = 16
NEGATIVE = -1e30
EPSILON = 1e-05
THETA = 10000.0
BF = jnp.bfloat16
F32 = jnp.float32
MIB = 1024 * 1024

WIDE = 2 * D + 128
KEYS = D + 128
ROUNDS = ((1, 4, 4, 256), (8, 2, 2, 128), (4, 2, 1, 128))


def exchange(value, axis):
    return lax.all_to_all(value, axis, 0, 0, tiled=False)


def swap(value, step):
    return lax.ppermute(value, "seq", [(i, i ^ step) for i in range(N)])


def angle_tables():
    inverse = THETA ** (-np.arange(HEAD_DIM // 2, dtype=np.float64) / (HEAD_DIM // 2))
    near = np.arange(-TOK, TOK, dtype=np.float64)[:, None] * inverse[None, :]
    base = (TOK * np.arange(16, dtype=np.float64))[:, None] * inverse[None, :]

    def wide(angle):
        cosine, sine = np.cos(angle), np.sin(angle)
        return np.stack(
            [np.concatenate([cosine, cosine], -1), np.concatenate([-sine, sine], -1)]
        ).astype(np.float32)

    return wide(near), wide(base)


def mm(left, right):
    return lax.dot_general(left, right, (((1,), (0,)), ((), ())), preferred_element_type=F32)


def mm_nt(left, right):
    return lax.dot_general(left, right, (((1,), (1,)), ((), ())), preferred_element_type=F32)


def mm_tn(left, right):
    return lax.dot_general(left, right, (((0,), (0,)), ((), ())), preferred_element_type=F32)


def table_row(ids):
    return ((ids & 15) << 4) | (((ids >> 4) & 3) << 2) | (ids >> 6)


def hot_columns(ids_row):
    place = lax.broadcasted_iota(jnp.int32, (VOCAB, TOK), 0)
    return (place == table_row(ids_row)).astype(F32).astype(BF)


def turn_tables(near_ref, base_ref, rows, block):
    near_c, near_s = near_ref[0, rows, :], near_ref[1, rows, :]
    base_c, base_s = base_ref[0, pl.ds(block, 1), :], base_ref[1, pl.ds(block, 1), :]
    return near_c * base_c - near_s * base_s, near_s * base_c + near_c * base_s


def turn(value, cosine, sine):
    return value * cosine + pltpu.roll(value, HEAD_DIM // 2, 1) * sine


def turn_back(value, cosine, sine):
    return value * cosine - pltpu.roll(value, HEAD_DIM // 2, 1) * sine


def head(index):
    return slice(index * HEAD_DIM, (index + 1) * HEAD_DIM)


def split(value):
    high = value.astype(BF).astype(F32)
    return high, value - high


def tiles(value, scratch):
    for k in range(8):
        scratch[k : k + 1, :] = value[:, k * 128 : (k + 1) * 128]
    return scratch[...]


def halve(value, step, count, keep_ref, send_ref):
    bit = (lax.axis_index("seq") // step) % 2
    keep_ref[...] = value[pl.ds(pl.multiple_of(bit * count, count), count), :]
    send_ref[...] = value[pl.ds(pl.multiple_of((1 - bit) * count, count), count), :].astype(BF)


def tables_kernel(*refs):
    sources, result_ref = refs[:11], refs[11]
    prev_ref, near_ref, base_ref, ids_ref, gain_ref, emb, wk, wv, wq, do, wo = refs[12:23]
    tab, q_ref, k_ref, v_ref, ga_ref, kprev, vprev, vtab, gq, kg, vg, scaled, terms, out_ref, sems = refs[23:]
    kept = (emb, gain_ref, ids_ref, prev_ref, near_ref, base_ref, wk, wv, wq, do, wo)
    copies = [pltpu.make_async_copy(s, d, sems.at[i]) for i, (s, d) in enumerate(zip(sources, kept))]
    for copy in copies[:7]:
        copy.start()
    block = lax.axis_index("seq")
    place = lax.broadcasted_iota(jnp.int32, (VOCAB, VOCAB), 0)
    value = lax.broadcasted_iota(jnp.int32, (VOCAB, VOCAB), 1)
    order = (table_row(value) == place).astype(F32).astype(BF)
    copies[0].wait()
    copies[1].wait()
    copies[7].start()
    copies[8].start()
    inputs = mm(order, emb[...])
    recip = lax.rsqrt(jnp.mean(inputs * inputs, axis=-1, keepdims=True) + EPSILON)
    scaled[...] = inputs * recip
    normed = (scaled[...] * gain_ref[...]).astype(BF)

    for copy in copies[2:6]:
        copy.wait()
    hot_own, hot_prev = hot_columns(ids_ref[...]), hot_columns(prev_ref[...])
    rows_own, rows_prev = hot_own.T, hot_prev.T
    cos_p, sin_p = turn_tables(near_ref, base_ref, slice(0, TOK), block)
    cos_o, sin_o = turn_tables(near_ref, base_ref, slice(TOK, 2 * TOK), block)

    def fill(weight):
        full = mm(normed, weight[...])
        high = full.astype(BF)
        tab[:VOCAB, :] = high
        tab[VOCAB:, :] = (full - high.astype(F32)).astype(BF)

    def gather(hot, cosine, sine, out_ref):
        full = mm(jnp.concatenate([hot, hot], axis=1), tab[...])
        for h in range(HEADS):
            out_ref[:, head(h)] = turn(full[:, head(h)], cosine, sine).astype(BF)

    copies[6].wait()
    copies[9].start()
    copies[10].start()
    fill(wk)
    gather(rows_own, cos_o, sin_o, k_ref)
    gather(rows_prev, cos_p, sin_p, kprev)
    copies[7].wait()
    vtab[...] = mm(normed, wv[...]).astype(BF)
    v_ref[...] = mm(rows_own, vtab[...]).astype(BF)
    vprev[...] = mm(rows_prev, vtab[...]).astype(BF)
    copies[8].wait()
    fill(wq)
    gather(rows_own, cos_o, sin_o, q_ref)
    copies[9].wait()
    copies[10].wait()
    ga_ref[...] = mm(do[...], wo[...]).astype(BF)
    lead = jnp.where(block == 0, NEGATIVE, 0.0).astype(F32)
    scale = HEAD_DIM ** (-0.5)
    own = lax.broadcasted_iota(jnp.int32, (TOK, TOK), 0) <= lax.broadcasted_iota(
        jnp.int32, (TOK, TOK), 1
    )
    behind_o = own.astype(F32).T.astype(BF)
    behind_p = 1 - behind_o
    for h in range(HEADS):
        query, grad = q_ref[:, head(h)], ga_ref[:, head(h)]
        key_o, key_p = k_ref[:, head(h)], kprev[:, head(h)]
        value_o, value_p = v_ref[:, head(h)], vprev[:, head(h)]
        scores = jnp.where(own, mm_nt(key_o, query), mm_nt(key_p, query) + lead)
        highest = jnp.max(scores, axis=0, keepdims=True)
        weights = jnp.exp((scores - highest) * scale)
        probs = weights * (1.0 / jnp.sum(weights, axis=0, keepdims=True))
        grad_probs = jnp.where(own, mm_nt(value_o, grad), mm_nt(value_p, grad))
        delta = jnp.sum(probs * grad_probs, axis=0, keepdims=True)
        grad_scores = probs * (grad_probs - delta) * scale
        probs_o = jnp.where(own, probs, 0.0).astype(BF)
        probs_p = jnp.where(own, 0.0, probs).astype(BF)
        gs_o = jnp.where(own, grad_scores, 0.0).astype(BF)
        gs_p = jnp.where(own, 0.0, grad_scores).astype(BF)
        turned = grad_scores.astype(BF).T
        vg[:TOK, head(h)] = mm(probs_p, grad).astype(BF)
        vg[TOK:, head(h)] = mm(probs_o, grad).astype(BF)
        kg[:TOK, head(h)] = turn_back(mm(gs_p, query), cos_p, sin_p).astype(BF)
        kg[TOK:, head(h)] = turn_back(mm(gs_o, query), cos_o, sin_o).astype(BF)
        grad_q = mm(turned * behind_o, key_o) + mm(turned * behind_p, key_p)
        gq[:, head(h)] = turn_back(grad_q, cos_o, sin_o).astype(BF)
    hot2 = jnp.concatenate([hot_prev, hot_own], axis=1)
    key_table = mm(hot2, kg[...]).astype(BF)
    out_ref[:, :, :D] = key_table.reshape(N, N, D)
    parts = [slice(0, D), slice(D, WIDE)]
    leaving = [
        pltpu.make_async_copy(out_ref.at[:, :, part], result_ref.at[:, :, part], sems.at[11 + i])
        for i, part in enumerate(parts)
    ]
    leaving[0].start()
    value_table = mm(hot2, vg[...]).astype(BF)
    query_table = mm(hot_own, gq[...]).astype(BF)
    grad_normed = mm_nt(key_table, wk[...]) + mm_nt(value_table, wv[...]) + mm_nt(query_table, wq[...])
    out_ref[:, :, D : 2 * D] = grad_normed.astype(BF).reshape(N, N, D)
    product = jnp.sum(grad_normed * scaled[...], axis=0, keepdims=True)
    gain_terms = jnp.concatenate(split(tiles(product, terms)), axis=0).astype(BF)
    out_ref[:, :, 2 * D :] = jnp.broadcast_to(gain_terms[None], (N, N, 128))
    leaving[1].start()
    for copy in leaving:
        copy.wait()


def rows_kernel(emb_ref, gain_ref, pick_ref, row_ref):
    block, lane = lax.axis_index("seq"), lax.axis_index("dp")
    index = lax.broadcasted_iota(jnp.int32, (2 * N, VOCAB), 0)
    value = lax.broadcasted_iota(jnp.int32, (2 * N, VOCAB), 1)
    wanted = jnp.where(index < N, N * lane + index, table_row(N * block + lane))
    inputs = mm((table_row(value) == wanted).astype(F32).astype(BF), emb_ref[...])
    recip = lax.rsqrt(jnp.mean(inputs * inputs, axis=-1, keepdims=True) + EPSILON)
    normed = (inputs * recip * gain_ref[...]).astype(BF)
    place = lax.broadcasted_iota(jnp.int32, (D, 128), 1)
    column = block * 64 + ((place >> 3) << 2) + (place & 3)
    choose = (lax.broadcasted_iota(jnp.int32, (D, 128), 0) == column).astype(F32).astype(BF)
    picked = mm(normed, choose)[:N]
    pick_ref[...] = jnp.concatenate([picked, picked], axis=0).astype(BF)
    row_ref[...] = inputs[N : N + 1]


def pack(rows, width):
    parts = [rows[:, k : k + width] for k in range(0, D, width)]
    if len(parts) * rows.shape[0] < N:
        parts.append(jnp.zeros((N - len(parts) * rows.shape[0], width), F32))
    return jnp.concatenate(parts, axis=0)


def unpack(packed, count, width):
    return jnp.concatenate([packed[k * count : (k + 1) * count] for k in range(D // width)], axis=1)


def share(keys_ref, grads, turn_of, kept_ref, sends):
    unit, ways, count, width = turn_of
    high, low = split(keys_ref[:8, D:] + keys_ref[8:, D:])
    keys_ref[:8, D:] = high
    keys_ref[8:, D:] = low
    place = (lax.axis_index("seq") // unit) % ways
    parts = [grads[k * count : (k + 1) * count] for k in range(ways)]

    def part(index):
        chosen = parts[0]
        for k in range(1, ways):
            chosen = jnp.where(index == k, parts[k], chosen)
        return chosen

    kept_ref[...] = part(place)
    keys = keys_ref[...].astype(BF)
    for k, send_ref in enumerate(sends):
        send_ref[:, :KEYS] = keys
        send_ref[:, KEYS:] = pack(part(place ^ (k + 1)), width).astype(BF)


def first_kernel(got_ref, keys_ref, kept_ref, *sends):
    total = jnp.sum(got_ref[...].astype(F32), axis=0)
    keys_ref[:, :D] = total[:, :D]
    keys_ref[:, D:] = total[:, 2 * D :]
    share(keys_ref, total[:, D : 2 * D], ROUNDS[0], kept_ref, sends)


def key_sum(keys_ref, got, columns):
    return sum((ref[:, columns].astype(F32) for ref in got), keys_ref[:, columns])


def grad_sum(kept_ref, got, turn_of):
    return sum((unpack(ref[:, KEYS:].astype(F32), *turn_of[2:]) for ref in got), kept_ref[...])


def round_kernel(index, old_ref, kept_ref, *refs):
    others = ROUNDS[index][1] - 1
    got, keys_ref, next_ref, sends = refs[:others], refs[others], refs[others + 1], refs[others + 2 :]
    keys_ref[...] = key_sum(old_ref, got, slice(0, KEYS))
    share(keys_ref, grad_sum(kept_ref, got, ROUNDS[index]), ROUNDS[index + 1], next_ref, sends)


def weight_kernel(keys_ref, *refs):
    got, (pick_ref, out_ref) = refs[:-2], refs[-2:]
    both = jnp.concatenate(split(key_sum(keys_ref, got, slice(0, D))), axis=0).astype(BF)
    part = mm_tn(pick_ref[...], both)
    first = (lax.broadcasted_iota(jnp.int32, (128, 512), 0) & 4) == 0
    out_ref[...] = jnp.where(first, part[:, :512], part[:, 512:]).reshape(N, 8, 512).astype(BF)


def row_kernel(keys_ref, kept_ref, *refs):
    got, (row_ref, gain_ref, ge_ref, gg_ref, sums) = refs[:-5], refs[-5:]
    sums[...] = key_sum(keys_ref, got, slice(D, KEYS))
    grad_normed = grad_sum(kept_ref, got, ROUNDS[-1])
    inputs = row_ref[...]
    recip = lax.rsqrt(jnp.mean(inputs * inputs, axis=-1, keepdims=True) + EPSILON)
    grad_scaled = grad_normed * gain_ref[...]
    inner = jnp.mean(grad_scaled * inputs, axis=-1, keepdims=True)
    ge_ref[...] = recip * grad_scaled - inputs * (recip * recip * recip) * inner
    terms = sums[:8] + sums[8:]
    start = (lax.axis_index("seq") * N + lax.axis_index("dp")) * 4
    mine = lax.broadcasted_iota(jnp.int32, (8, 128), 0) == start // 128
    row = jnp.sum(jnp.where(mine, terms, 0.0), axis=0, keepdims=True)
    gg_ref[...] = pltpu.roll(jnp.broadcast_to(row, (8, 128)), 128 - lax.rem(start, 128), 1)


def finish_kernel(got_ref, gk_ref):
    total = jnp.sum(got_ref[...].astype(F32), axis=0)
    gk_ref[:, :512] = total[:4]
    gk_ref[:, 512:] = total[4:]


def call(kernel, outs, ins, scratch=(), flops=0, moved=0, limit=16, far_out=False):
    far_space = pl.BlockSpec(memory_space=pl.ANY)
    vmem = pl.BlockSpec(memory_space=pltpu.VMEM)
    return pl.pallas_call(
        kernel,
        out_shape=[jax.ShapeDtypeStruct(shape, kind) for shape, kind in outs],
        in_specs=[far_space if far else vmem for _, far in ins],
        out_specs=[far_space if far_out else vmem] * len(outs),
        scratch_shapes=list(scratch),
        compiler_params=pltpu.CompilerParams(vmem_limit_bytes=limit * MIB),
        cost_estimate=pl.CostEstimate(flops=flops, bytes_accessed=moved, transcendentals=0),
    )(*[value for value, _ in ins])


def local(byte_ids, embedding, gain, w_query, w_key, w_value, w_out, d_output):
    near_table, base_table = (jnp.asarray(table) for table in angle_tables())
    prev_ids = lax.ppermute(byte_ids, "seq", [(i, i + 1) for i in range(N - 1)])
    gain_row = gain.reshape(1, D)
    mat = pltpu.VMEM((D, D), BF)
    tall = pltpu.VMEM((2 * TOK, D), BF)
    flat = pltpu.VMEM((TOK, D), BF)
    near = lambda *values: [(value, False) for value in values]
    far = lambda *values: [(value, True) for value in values]
    (tables,) = call(
        tables_kernel,
        [((N, N, WIDE), BF)],
        far(embedding, gain_row, byte_ids, prev_ids, near_table, base_table)
        + far(w_key, w_value, w_query, d_output[0], w_out),
        [
            pltpu.VMEM((1, TOK), jnp.int32),
            pltpu.VMEM((2, 2 * TOK, 128), F32),
            pltpu.VMEM((2, N, 128), F32),
            pltpu.VMEM((1, TOK), jnp.int32),
            pltpu.VMEM((1, D), F32),
            *[flat, mat, mat, mat, flat, mat, tall],
            *[flat] * 8,
            *[tall, tall],
            pltpu.VMEM((VOCAB, D), F32),
            pltpu.VMEM((8, 128), F32),
            pltpu.VMEM((N, N, WIDE), BF),
            pltpu.SemaphoreType.DMA((13,)),
        ],
        flops=8_000_000_000,
        moved=14_000_000,
        limit=56,
        far_out=True,
    )
    parts = exchange(tables, "dp")
    embedding_later, _ = lax.optimization_barrier((embedding, tables))
    pick, row = call(
        rows_kernel,
        [((32, 128), BF), ((1, D), F32)],
        near(embedding_later, gain_row),
        flops=10_000_000,
        moved=600_000,
    )
    def held(unit, ways, count, width):
        return [((N, KEYS), F32), ((count, D), F32)] + [((N, KEYS + width), BF)] * (ways - 1)

    def spread(sends, unit):
        return [swap(value, unit * (k + 1)) for k, value in enumerate(sends)]

    keys, kept, *sends = call(
        first_kernel, held(*ROUNDS[0]), near(parts), flops=1_000_000, moved=1_300_000
    )
    for index in range(len(ROUNDS) - 1):
        keys, kept, *sends = call(
            functools.partial(round_kernel, index),
            held(*ROUNDS[index + 1]),
            near(keys, kept, *spread(sends, ROUNDS[index][0])),
            flops=1_000_000,
            moved=400_000,
        )
    got = spread(sends, ROUNDS[-1][0])
    (part,) = call(
        weight_kernel, [((N, 8, 512), BF)], near(keys, *got, pick), flops=10_000_000, moved=400_000
    )
    parts = exchange(part, "dp")
    grad_row, gain_own = call(
        row_kernel,
        [((1, D), F32), ((8, 128), F32)],
        near(keys, kept, *got, row, gain_row),
        [pltpu.VMEM((N, 128), F32)],
        flops=1_000_000,
        moved=200_000,
    )
    (grad_weight,) = call(finish_kernel, [((4, D), F32)], near(parts), flops=1_000_000, moved=200_000)
    return grad_weight, gain_own[0, :4], grad_row


def solution(mesh):
    in_specs = (P("dp", "seq"), P(), P(), P(), P(), P(), P(), P("dp", "seq", None))
    out_specs = (P(("seq", "dp"), None), P(("seq", "dp")), P(("seq", "dp"), None))
    return jax.shard_map(local, mesh=mesh, in_specs=in_specs, out_specs=out_specs, check_vma=False)
```
